32 devices in a mesh: row: 8 (over y, x, core), col: 4 (over z).
Axes of the slice: x: 2, y: 2, z: 4, core: 2. Of those that a mesh axis runs over, the one named last changes fastest.
Arguments:
- vis: float32 [2, 262144], P(None, ('row', 'col')), may hold values from -6 to 6
- vis_pos: int32 [2, 262144], P(None, ('row', 'col')), may hold values from 0 to 199
- vis_w: int32 [262144], P(('row', 'col')), may hold values from 0 to 1023
- subgrid_tile: int32 [1024, 1], P(('row', 'col')), may hold values from 0 to 3; in each aligned block of 32 rows (0 to 31, 32 to 63, ...) at most 16 rows name the same one
- subgrid_group: int32 [1024, 1], P(('row', 'col')), may hold values from 0 to 3; in each aligned block of 32 rows (0 to 31, 32 to 63, ...) at most 12 rows name the same one
- subgrid_col: int32 [1024], P(('row', 'col')), may hold values from 0 to 2016
- grid_kernel: float32 [8, 8], replicated, may hold values from 0.1 to 1
- scale_kernels: float32 [2, 33], replicated, may hold values from -1 to 1
Outputs:
- scale_images: float32 [2, 8192, 8192], P(None, ('row', 'col'))
The draws below stay inside these ranges and needn't reach their ends.
Inputs may be any that keep to these rules, and one draw needn't show every extreme that they name: `vis_pos`: row 0 counts along grid rows, row 1 along grid columns, in steps of 1/8 cell from the corner of the visibility's subgrid. `subgrid_tile`: among the subgrids of one device (aligned blocks of 32), at most 16 name the same column tile; in some blocks one tile is named exactly that often. `subgrid_group`: among the subgrids of one device (aligned blocks of 32), at most 12 name the same row group; in some blocks one group is named exactly that often.
All inputs are finite; a program needn't handle non-finite values.
Results may differ from the reference program's by a relative error of at most 0.0003.
Values sent between devices are 32-bit elements; how exact they have to be, the bound alone decides.
No kernel may reach another device: no remote copies, remote signals or barrier semaphores. Data moves between devices by JAX's collectives and lax.ppermute only.
A program may use at most 128 MiB of HBM per device.

```python
import math
import jax
import jax.numpy as jnp
import numpy as np
from jax import lax

G = 8192
SUB = 32
SUP = 8
OVER = 8
VPS = 256
WSTEPS = 1024
KW = 33
NSCALE = 2
SUBS_DEV = 32
SUBS = 1024
VIS = 262144
TC = 2048
NGRP = 4
CAPT = 16
MOSTG = 12
N_ROW = 8
N_COL = 4


def touch_ends(drawn, own_key, smallest, largest):
    place = [jax.random.randint(jax.random.fold_in(own_key, axis), (), 0, length) for axis, length in enumerate(drawn.shape)]
    main_axis = drawn.shape.index(max(drawn.shape))
    neighbour = place[:main_axis] + [(place[main_axis] + 1) % drawn.shape[main_axis]] + place[main_axis + 1:]
    return drawn.at[tuple(place)].set(smallest).at[tuple(neighbour)].set(largest)


def shard_levels(stream_key, shape, pieces, smallest, largest):
    def one(axis_at, blocks):
        heights = jax.random.uniform(jax.random.fold_in(jax.random.fold_in(stream_key, 6), axis_at), (blocks,), jnp.float32, smallest / len(pieces), largest / len(pieces))
        return jnp.repeat(jnp.exp(heights), shape[axis_at] // blocks).reshape((-1,) + (1,) * (len(shape) - axis_at - 1))

    level = one(*pieces[0])
    for cut in pieces[1:]:
        level = level * one(*cut)
    return level


def deal_out(stream_key, own, number, rows, amount, top, most, lean):
    ranking = jax.random.permutation(stream_key, amount)
    packed, usual = portions_of(amount, rows * top, most, lean, True), portions_of(amount, rows * top, most, lean, False)
    places = jnp.arange(amount)

    def named(lengths, offset_by):
        used = int((lengths > 0).sum())
        fixed = max(1, used // 4)
        passed = fixed + (places - fixed + offset_by * (used - fixed)) % max(1, amount - fixed)
        return jnp.zeros((amount,), jnp.int32).at[ranking[jnp.where(places < fixed, places, passed)]].set(jnp.asarray(lengths, jnp.int32))

    lengths = jnp.where(number % 4 == 0, named(packed, number // 4), named(usual, number - number // 4 - 1))
    mixed = jax.random.permutation(jax.random.fold_in(own, 3), amount)
    donor, sink = mixed[0:amount // 2 * 2:2], mixed[1:amount // 2 * 2:2]
    margin = jnp.minimum(lengths[donor] - 1, most - lengths[sink]) // 2
    margin = jnp.where((donor == ranking[0]) | (sink == ranking[0]) | (lengths[sink] == 0), 0, jnp.maximum(margin, 0))
    passed = jax.random.randint(jax.random.fold_in(own, 4), (amount // 2,), 0, 1 << 20) % (margin + 1)
    lengths = lengths.at[donor].add(-passed).at[sink].add(passed)
    items = jnp.searchsorted(jnp.cumsum(lengths), jnp.arange(rows * top), side="right").astype(jnp.int32)
    listing = items.reshape(top, rows).T
    listing = listing[jax.random.permutation(jax.random.fold_in(own, 1), rows)]
    offset_by = jax.random.randint(jax.random.fold_in(own, 2), (rows, 1), 0, top)
    return jnp.take_along_axis(listing, (jnp.arange(top)[None, :] + offset_by) % top, axis=1)


def portions_of(amount, total, bound, slope, full):
    weights = [(1 << 20) // math.isqrt(rank ** slope) + 1 for rank in range(1, amount + 1)]
    largest = bound if full else min(bound, max(-(-total // amount), total * weights[0] // sum(weights)))
    least = 1 if total - largest >= amount - 1 else 0
    counts, rest = [largest] + [least] * (amount - 1), total - largest - least * (amount - 1)
    while rest > 0:
        candidates = [i for i in range(1, amount) if counts[i] < largest] or [i for i in range(1, amount) if counts[i] < bound]
        mass, left = sum([weights[i] for i in candidates]), rest
        for i in candidates:
            more = min(bound - counts[i], max(1, left * weights[i] // mass), rest)
            counts[i] = counts[i] + more
            rest = rest - more
    return np.array(counts)


def gaussian(key, shape, scale, most, split=(), kind=jnp.bfloat16):
    values = jax.random.normal(key, shape, jnp.float32) * scale
    if len(split) > 0:
        values = shard_levels(key, shape, split, -0.22, 0.18) * values
    return jnp.clip(values, min=-most, max=most).astype(kind)


def setup_inputs(seed: int = 0) -> dict:
    keys = jax.random.split(jax.random.key(seed), 9)
    vis = gaussian(keys[0], (2, VIS), 1.0, 6.0, ((1, 32),), jnp.float32)
    vis_pos = touch_ends(jax.random.randint(keys[1], (2, VIS), 0, (SUB - SUP + 1) * OVER), jax.random.fold_in(keys[1], 1), 0, ((SUB - SUP + 1) * OVER) - 1).astype(jnp.int32)
    vis_w = touch_ends(jax.random.randint(keys[2], (VIS,), 0, WSTEPS), jax.random.fold_in(keys[2], 1), 0, WSTEPS - 1).astype(jnp.int32)
    subgrid_tile_keys = jax.random.split(jax.random.fold_in(keys[3], 1), SUBS // SUBS_DEV)
    subgrid_tile_turns = jax.random.permutation(jax.random.fold_in(keys[3], 3), SUBS // SUBS_DEV)
    subgrid_tile = jax.vmap(lambda own, number: deal_out(jax.random.fold_in(keys[3], 2), own, number, SUBS_DEV, N_COL, 1, CAPT, 2))(subgrid_tile_keys, subgrid_tile_turns).reshape((SUBS, 1))
    subgrid_group_keys = jax.random.split(jax.random.fold_in(keys[4], 1), SUBS // SUBS_DEV)
    subgrid_group_turns = jax.random.permutation(jax.random.fold_in(keys[4], 3), SUBS // SUBS_DEV)
    subgrid_group = jax.vmap(lambda own, number: deal_out(jax.random.fold_in(keys[4], 2), own, number, SUBS_DEV, NGRP, 1, MOSTG, 1))(subgrid_group_keys, subgrid_group_turns).reshape((SUBS, 1))
    subgrid_col = touch_ends(jax.random.randint(keys[5], (SUBS,), 0, TC - SUB + 1), jax.random.fold_in(keys[5], 1), 0, TC - SUB).astype(jnp.int32)
    grid_kernel = jnp.clip(jnp.exp(jax.random.uniform(keys[6], (OVER, SUP), jnp.float32, math.log(0.1), math.log(1.0))), 0.1, 1.0)
    scale_kernels = gaussian(keys[7], (NSCALE, KW), KW ** -0.5, 1.0, (), jnp.float32)
    return {"vis": vis, "vis_pos": vis_pos, "vis_w": vis_w, "subgrid_tile": subgrid_tile, "subgrid_group": subgrid_group, "subgrid_col": subgrid_col, "grid_kernel": grid_kernel, "scale_kernels": scale_kernels}


HIGHEST = lax.Precision.HIGHEST


def kernel_taps(positions, grid_kernel):
    cell_index = positions // OVER
    fraction = positions % OVER
    onehot = (fraction[:, None] == jnp.arange(OVER, dtype=jnp.int32)[None, :]).astype(grid_kernel.dtype)
    values = jnp.dot(onehot, grid_kernel, precision=HIGHEST)
    offset = jnp.arange(SUB, dtype=jnp.int32)[None, :] - cell_index[:, None]
    result = jnp.zeros(offset.shape, grid_kernel.dtype)
    for tap_index in range(SUP):
        result = result + jnp.where(offset == tap_index, values[:, tap_index:tap_index + 1], 0.0)
    return result


def make_subgrids(vis_block, pos_block, phase_steps, grid_kernel, number):
    along_rows = kernel_taps(pos_block[0], grid_kernel).reshape(number, VPS, SUB)
    along_cols = kernel_taps(pos_block[1], grid_kernel).reshape(number, VPS, SUB)
    angles = phase_steps.astype(grid_kernel.dtype) * (2.0 * math.pi / WSTEPS)
    cosine = jnp.cos(angles)
    sine_part = jnp.sin(angles)
    rotated_real = vis_block[0] * cosine + vis_block[1] * sine_part
    rotated_imag = vis_block[1] * cosine - vis_block[0] * sine_part
    weighted_real = along_rows * rotated_real.reshape(number, VPS, 1)
    weighted_imag = along_rows * rotated_imag.reshape(number, VPS, 1)
    sub_real = jnp.einsum('sja,sjb->sab', weighted_real, along_cols, precision=HIGHEST)
    sub_imag = jnp.einsum('sja,sjb->sab', weighted_imag, along_cols, precision=HIGHEST)
    return sub_real, sub_imag


def reference(vis, vis_pos, vis_w, subgrid_tile, subgrid_group, subgrid_col, grid_kernel, scale_kernels):
    band_rows = G // N_ROW
    tile_width = G // N_COL
    group_rows = band_rows // N_COL
    per_device = SUBS_DEV * VPS
    cell_offsets = (jnp.arange(SUB, dtype=jnp.int32)[:, None] * G + jnp.arange(SUB, dtype=jnp.int32)[None, :]).reshape(-1)

    def add_device(carry, device):
        grid_real, grid_imag = carry
        start = device * per_device
        vis_block = lax.dynamic_slice_in_dim(vis, start, per_device, 1)
        pos_block = lax.dynamic_slice_in_dim(vis_pos, start, per_device, 1)
        phase_block = lax.dynamic_slice_in_dim(vis_w, start, per_device, 0)
        first_sub = device * SUBS_DEV
        tile_index = lax.dynamic_slice_in_dim(subgrid_tile[:, 0], first_sub, SUBS_DEV, 0)
        groups = lax.dynamic_slice_in_dim(subgrid_group[:, 0], first_sub, SUBS_DEV, 0)
        columns = lax.dynamic_slice_in_dim(subgrid_col, first_sub, SUBS_DEV, 0)
        band_index = device // N_COL
        corner_row = band_index * band_rows + groups * group_rows
        corner_col = tile_index * tile_width + columns
        sub_real, sub_imag = make_subgrids(vis_block, pos_block, phase_block, grid_kernel, SUBS_DEV)
        targets = ((corner_row * G + corner_col)[:, None] + cell_offsets[None, :]).reshape(-1)
        grid_real = grid_real.at[targets].add(sub_real.reshape(-1))
        grid_imag = grid_imag.at[targets].add(sub_imag.reshape(-1))
        return (grid_real, grid_imag), None

    zeros = jnp.zeros((G * G,), vis.dtype)
    (grid_real, grid_imag), unused = lax.scan(add_device, (zeros, zeros), jnp.arange(N_ROW * N_COL, dtype=jnp.int32))
    grid = lax.complex(grid_real, grid_imag).reshape(G, G)
    image = jnp.real(jnp.fft.ifft2(grid)) * G
    image = image.T
    halo_width = (KW - 1) // 2
    vertical = lax.conv_general_dilated(image[None, None], scale_kernels[:, None, None, :], (1, 1), ((0, 0), (halo_width, halo_width)), precision=HIGHEST)
    smoothed = lax.conv_general_dilated(vertical, scale_kernels[:, None, :, None], (1, 1), ((halo_width, halo_width), (0, 0)), feature_group_count=NSCALE, precision=HIGHEST)
    return smoothed[0]
```

```python
import math

import jax
import jax.numpy as jnp
import numpy as np
from jax import lax
from jax.experimental import pallas as pl
from jax.experimental.pallas import tpu as pltpu
from jax.sharding import PartitionSpec as P

G = 8192
SUB = 32
SUP = 8
OVER = 8
VPS = 256
WSTEPS = 1024
KW = 33
NSCALE = 2
HALO = (KW - 1) // 2
RADIX = 8
LANES = 128

HIGHEST = lax.Precision.HIGHEST
F32 = jnp.float32
BF16 = jnp.bfloat16
ROOT_HALF = math.sqrt(0.5)


def with_halo(array, sides, width):
    for axis, dim in sides:
        count, length = (lax.axis_size(axis), array.shape[dim])
        up = [(i, (i + 1) % count) for i in range(count - 1)]
        down = [(j, i) for i, j in up]
        last = lax.slice_in_dim(array, length - width, length, axis=dim)
        initial = lax.slice_in_dim(array, 0, width, axis=dim)
        before = lax.ppermute(last, axis, up)
        after = lax.ppermute(initial, axis, down)
        array = jnp.concatenate([before, array, after], axis=dim)
    return array


def kernel_taps(positions, grid_kernel):
    cell_index = positions // OVER
    fraction = positions % OVER
    onehot = (fraction[:, None] == jnp.arange(OVER, dtype=jnp.int32)[None, :]).astype(
        grid_kernel.dtype
    )
    values = jnp.dot(onehot, grid_kernel, precision=HIGHEST)
    offset = jnp.arange(SUB, dtype=jnp.int32)[None, :] - cell_index[:, None]
    result = jnp.zeros(offset.shape, grid_kernel.dtype)
    for tap_index in range(SUP):
        result = result + jnp.where(offset == tap_index, values[:, tap_index : tap_index + 1], 0.0)
    return result


def rotated_visibilities(vis_block, phase_steps):
    angles = phase_steps.astype(vis_block.dtype) * (2.0 * math.pi / WSTEPS)
    cosine = jnp.cos(angles)
    sine_part = jnp.sin(angles)
    return (
        vis_block[0] * cosine + vis_block[1] * sine_part,
        vis_block[1] * cosine - vis_block[0] * sine_part,
    )


def make_subgrids(vis_block, pos_block, phase_steps, grid_kernel, number):
    along_rows = kernel_taps(pos_block[0], grid_kernel).reshape(number, VPS, SUB)
    along_cols = kernel_taps(pos_block[1], grid_kernel).reshape(number, VPS, SUB)
    rotated_real, rotated_imag = rotated_visibilities(vis_block, phase_steps)
    weighted_real = along_rows * rotated_real.reshape(number, VPS, 1)
    weighted_imag = along_rows * rotated_imag.reshape(number, VPS, 1)
    sub_real = jnp.einsum("sja,sjb->sab", weighted_real, along_cols, precision=HIGHEST)
    sub_imag = jnp.einsum("sja,sjb->sab", weighted_imag, along_cols, precision=HIGHEST)
    return (sub_real, sub_imag)


def dft_table(length):
    positions = jnp.arange(length, dtype=jnp.int32)
    product = positions[:, None] * positions[None, :] % length
    angles = product.astype(jnp.float32) * (2.0 * math.pi / length)
    return (jnp.cos(angles), jnp.sin(angles))


def transform_last(real_part, imag_part, real_only):
    length = real_part.shape[-1]
    factor_one = 2 ** ((length.bit_length() - 1) // 2)
    factor_two = length // factor_one
    leading = real_part.shape[:-1]
    real_part = real_part.reshape(leading + (factor_one, factor_two))
    imag_part = imag_part.reshape(leading + (factor_one, factor_two))
    cos_one, sin_one = dft_table(factor_one)
    section_real = jnp.einsum(
        "...ab,ak->...kb", real_part, cos_one, precision=HIGHEST
    ) - jnp.einsum("...ab,ak->...kb", imag_part, sin_one, precision=HIGHEST)
    section_imag = jnp.einsum(
        "...ab,ak->...kb", real_part, sin_one, precision=HIGHEST
    ) + jnp.einsum("...ab,ak->...kb", imag_part, cos_one, precision=HIGHEST)
    outer_index = (
        jnp.arange(factor_one, dtype=jnp.int32)[:, None]
        * jnp.arange(factor_two, dtype=jnp.int32)[None, :]
        % length
    )
    twiddle = outer_index.astype(jnp.float32) * (2.0 * math.pi / length)
    twiddle_cos = jnp.cos(twiddle)
    twiddle_sin = jnp.sin(twiddle)
    turned_real = section_real * twiddle_cos - section_imag * twiddle_sin
    turned_imag = section_real * twiddle_sin + section_imag * twiddle_cos
    cos_two, sin_two = dft_table(factor_two)
    result_real = jnp.einsum(
        "...kb,bq->...qk", turned_real, cos_two, precision=HIGHEST
    ) - jnp.einsum("...kb,bq->...qk", turned_imag, sin_two, precision=HIGHEST)
    result_real = result_real.reshape(leading + (length,))
    if real_only:
        return result_real
    result_imag = jnp.einsum(
        "...kb,bq->...qk", turned_real, sin_two, precision=HIGHEST
    ) + jnp.einsum("...kb,bq->...qk", turned_imag, cos_two, precision=HIGHEST)
    return (result_real, result_imag.reshape(leading + (length,)))


def band_matrix(kernel_row, height, columns):
    distance = (
        jnp.arange(height, dtype=jnp.int32)[:, None] - jnp.arange(columns, dtype=jnp.int32)[None, :]
    )
    matrix = jnp.zeros((height, columns), jnp.float32)
    for tap_index in range(KW):
        matrix = matrix + jnp.where(distance == tap_index, kernel_row[tap_index], 0.0)
    return matrix


def smooth_along_rows(field, kernel_row):
    height = field.shape[0]
    length = field.shape[1]
    halo_width = (KW - 1) // 2
    block_size = min(128, length)
    blocks = length // block_size
    padded = jnp.pad(field, ((0, 0), (halo_width, block_size - halo_width)))
    framed = padded.reshape(height, blocks + 1, block_size)
    windows = jnp.concatenate([framed[:, :-1, :], framed[:, 1:, : 2 * halo_width]], axis=2)
    matrix = band_matrix(kernel_row, block_size + 2 * halo_width, block_size)
    return jnp.einsum("rni,io->rno", windows, matrix, precision=HIGHEST).reshape(height, length)


def smooth_across(field, kernel_row):
    height = field.shape[0]
    inner_rows = height - (KW - 1)
    matrix = band_matrix(kernel_row, height, inner_rows)
    return jnp.einsum("ry,rx->xy", field, matrix, precision=HIGHEST)


def slot_numbers(bucket_keys, buckets, capacity):
    count = bucket_keys.shape[0]
    index = jnp.arange(count, dtype=jnp.int32)
    same = (bucket_keys[:, None] == bucket_keys[None, :]) & (index[None, :] < index[:, None])
    return bucket_keys * capacity + jnp.sum(same.astype(jnp.int32), axis=1)


def place_blocks(piece_real, piece_imag, owner, start, buckets, width):
    count = piece_real.shape[0]
    piece_rows = piece_real.shape[1] // SUB
    step = math.gcd(count, 32)
    turns = count // step
    piece_real = piece_real.reshape(turns, step, piece_rows, SUB)
    piece_imag = piece_imag.reshape(turns, step, piece_rows, SUB)
    owner = owner.reshape(turns, step)
    start = start.reshape(turns, step)
    column_index = jnp.arange(width, dtype=jnp.int32)
    sub_index = jnp.arange(SUB, dtype=jnp.int32)
    bucket_index = jnp.arange(buckets, dtype=jnp.int32)

    def add_block(carry, block):
        block_real, block_imag, block_owner, block_start = block
        shift = (
            column_index[None, None, :] == block_start[:, None, None] + sub_index[None, :, None]
        ).astype(jnp.float32)
        pick = (block_owner[:, None] == bucket_index[None, :]).astype(jnp.float32)
        moved_real = jnp.einsum("sab,sbc->sac", block_real, shift, precision=HIGHEST)
        moved_imag = jnp.einsum("sab,sbc->sac", block_imag, shift, precision=HIGHEST)
        total_real = carry[0] + jnp.einsum("sg,sac->gac", pick, moved_real, precision=HIGHEST)
        total_imag = carry[1] + jnp.einsum("sg,sac->gac", pick, moved_imag, precision=HIGHEST)
        return ((total_real, total_imag), None)

    empty = jnp.zeros((buckets, piece_rows, width), jnp.float32)
    (placed_real, placed_imag), unused = lax.scan(
        add_block, (empty, empty), (piece_real, piece_imag, owner, start)
    )
    return (placed_real, placed_imag)


def general_device(
    vis, vis_pos, vis_w, subgrid_tile, subgrid_group, subgrid_col, grid_kernel, scale_kernels
):
    row_devices = lax.axis_size("row")
    col_devices = lax.axis_size("col")
    band_rows = G // row_devices
    tile_width = G // col_devices
    group_rows = band_rows // col_devices
    pencil_cols = G // (row_devices * col_devices)
    piece_rows = min(group_rows, SUB)
    pieces = SUB // piece_rows
    subgrids_here = subgrid_col.shape[0]
    batch_size = min(16, subgrids_here)
    batches = subgrids_here // batch_size
    batch_vis = batch_size * VPS

    def grid_batch(step_index):
        start = step_index * batch_vis
        vis_block = lax.dynamic_slice_in_dim(vis, start, batch_vis, 1)
        pos_block = lax.dynamic_slice_in_dim(vis_pos, start, batch_vis, 1)
        phase_block = lax.dynamic_slice_in_dim(vis_w, start, batch_vis, 0)
        sub_real, sub_imag = make_subgrids(
            vis_block, pos_block, phase_block, grid_kernel, batch_size
        )
        return (sub_real.reshape(batch_size, SUB * SUB), sub_imag.reshape(batch_size, SUB * SUB))

    sub_real, sub_imag = lax.map(grid_batch, jnp.arange(batches, dtype=jnp.int32))
    sub_real = sub_real.reshape(subgrids_here, SUB * SUB)
    sub_imag = sub_imag.reshape(subgrids_here, SUB * SUB)
    tile_index = subgrid_tile[:, 0]
    groups = subgrid_group[:, 0]
    groups_used = col_devices - pieces + 1
    most_group = min(subgrids_here, 3 * ((subgrids_here + groups_used - 1) // groups_used) // 2)
    capacity = pieces * most_group
    owners = (groups[:, None] + jnp.arange(pieces, dtype=jnp.int32)[None, :]).reshape(-1)
    starts = jnp.broadcast_to(
        (tile_index * tile_width + subgrid_col)[:, None], (subgrids_here, pieces)
    ).reshape(-1)
    slot_index = slot_numbers(owners, col_devices, capacity)
    piece_real = sub_real.reshape(subgrids_here * pieces, piece_rows * SUB)
    piece_imag = sub_imag.reshape(subgrids_here * pieces, piece_rows * SUB)
    send_real = (
        jnp.zeros((col_devices * capacity, piece_rows * SUB), jnp.float32)
        .at[slot_index]
        .set(piece_real)
    )
    send_imag = (
        jnp.zeros((col_devices * capacity, piece_rows * SUB), jnp.float32)
        .at[slot_index]
        .set(piece_imag)
    )
    send_start = jnp.zeros((col_devices * capacity,), jnp.int32).at[slot_index].set(starts)
    recv_real, recv_imag, recv_start = (
        lax.all_to_all(send_real, "col", split_axis=0, concat_axis=0, tiled=True),
        lax.all_to_all(send_imag, "col", split_axis=0, concat_axis=0, tiled=True),
        lax.all_to_all(send_start, "col", split_axis=0, concat_axis=0, tiled=True),
    )
    placed_real, placed_imag = place_blocks(
        recv_real,
        recv_imag,
        recv_start // tile_width,
        recv_start % tile_width,
        col_devices,
        tile_width,
    )
    widen = ((0, group_rows - piece_rows), (0, 0))
    slab_real = jnp.pad(placed_real.transpose(1, 0, 2).reshape(piece_rows, G), widen)
    slab_imag = jnp.pad(placed_imag.transpose(1, 0, 2).reshape(piece_rows, G), widen)
    rows_real, rows_imag = transform_last(slab_real, slab_imag, False)
    cols_real, cols_imag = (
        lax.all_to_all(
            lax.all_to_all(rows_real, "row", split_axis=1, concat_axis=0, tiled=True),
            "col",
            split_axis=1,
            concat_axis=0,
            tiled=True,
        ),
        lax.all_to_all(
            lax.all_to_all(rows_imag, "row", split_axis=1, concat_axis=0, tiled=True),
            "col",
            split_axis=1,
            concat_axis=0,
            tiled=True,
        ),
    )

    def reorder(field):
        return (
            field.reshape(col_devices, row_devices, group_rows, pencil_cols)
            .transpose(3, 1, 0, 2)
            .reshape(pencil_cols, G)
        )

    image = transform_last(reorder(cols_real), reorder(cols_imag), True) * (1.0 / G)
    halo_width = (KW - 1) // 2
    results = []
    padded = with_halo(image, ((("row", "col"), 0),), halo_width)
    for scale_index in range(NSCALE):
        vertical = smooth_along_rows(padded, scale_kernels[scale_index])
        results.append(smooth_across(vertical, scale_kernels[scale_index]))
    return jnp.stack(results)


def split(value):
    high = value.astype(BF16)
    return high, (value - high.astype(F32)).astype(BF16)


def split_outside(value):
    high = lax.reduce_precision(value, 8, 7)
    return high.astype(BF16), (value - high).astype(BF16)


def split_table(table):
    table = np.asarray(table, np.float64)
    high = table.astype(BF16)
    return high, (table - high.astype(np.float64)).astype(BF16)


def turn(steps, length):
    angle = 2.0 * np.pi * (np.asarray(steps, np.int64) % length) / length
    return np.cos(angle), np.sin(angle)


def dot(left, right, left_dim=1, right_dim=0):
    return lax.dot_general(
        left, right, (((left_dim,), (right_dim,)), ((), ())), preferred_element_type=F32
    )


def dot3(left_high, left_low, right_high, right_low, left_dim=1, right_dim=0):
    return (
        dot(left_high, right_high, left_dim, right_dim)
        + dot(left_high, right_low, left_dim, right_dim)
        + dot(left_low, right_high, left_dim, right_dim)
    )


def subgrid_kernel(pos_ref, rot_ref, taps_ref, out_ref):
    span = 2 * VPS
    table = taps_ref[...]

    def taps(position):
        step = position & (OVER - 1)
        cell = position >> (OVER.bit_length() - 1)
        values = jnp.zeros((SUP, span), F32)
        for s in range(OVER):
            values = jnp.where(step == s, table[:, s : s + 1], values)
        offset = lax.broadcasted_iota(jnp.int32, (SUB, span), 0) - cell
        result = jnp.zeros((SUB, span), F32)
        for t in range(SUP):
            result = jnp.where(offset == t, values[t : t + 1, :], result)
        return result

    first = lax.broadcasted_iota(jnp.int32, (SUB, LANES), 1) < LANES // 2

    def pair(p, carry):
        here = pl.ds(pl.multiple_of(p * span, span), span)
        along_rows = taps(pos_ref[0:1, here])
        along_cols = taps(pos_ref[1:2, here])
        weighted = jnp.concatenate(
            [along_rows * rot_ref[0:1, here], along_rows * rot_ref[1:2, here]], axis=0
        )
        weighted = jnp.concatenate(split(weighted), axis=0)
        cols = jnp.concatenate(split(along_cols), axis=0)
        sums = []
        for s in range(2):
            part = slice(s * VPS, (s + 1) * VPS)
            product = dot(cols[:, part], weighted[:, part], 1, 1)
            total = product[:SUB] + product[SUB:]
            sums.append(total + pltpu.roll(total, LANES // 2, 1))
        out_ref[pl.ds(pl.multiple_of(p * SUB, SUB), SUB), :] = jnp.where(first, sums[0], sums[1])
        return carry

    lax.fori_loop(0, out_ref.shape[0] // SUB, pair, 0)


def radix_eight(real, imag):
    def four(r, i):
        a, b = (r[0] + r[2], i[0] + i[2])
        c, d = (r[0] - r[2], i[0] - i[2])
        e, f = (r[1] + r[3], i[1] + i[3])
        g, h = (r[1] - r[3], i[1] - i[3])
        return [(a + e, b + f), (c - h, d + g), (a - e, b - f), (c + h, d - g)]

    low = four(
        [real[n] + real[n + 4] for n in range(4)], [imag[n] + imag[n + 4] for n in range(4)]
    )
    dr = [real[n] - real[n + 4] for n in range(4)]
    di = [imag[n] - imag[n + 4] for n in range(4)]
    high = four(
        [dr[0], (dr[1] - di[1]) * ROOT_HALF, -di[2], (dr[3] + di[3]) * -ROOT_HALF],
        [di[0], (dr[1] + di[1]) * ROOT_HALF, dr[2], (dr[3] - di[3]) * ROOT_HALF],
    )
    return [(low, high)[c % 2][c // 2] for c in range(8)]


def row_kernel(
    info_ref, *refs, blocks, part, per_class
):
    xs = refs[:blocks]
    turn_ref, high_ref, low_ref, out_ref, real_ref, imag_ref, uh_ref, ul_ref = refs[blocks:]
    rows = real_ref.shape[0]
    chunk = 256

    def clear(n, carry):
        here = pl.ds(pl.multiple_of(n * chunk, chunk), chunk)
        real_ref[here, :] = jnp.zeros((chunk, LANES), F32)
        imag_ref[here, :] = jnp.zeros((chunk, LANES), F32)
        return carry

    lax.fori_loop(0, rows // chunk, clear, 0)
    owner = lax.broadcasted_iota(jnp.int32, (SUB, LANES), 1) // SUB
    for b in range(blocks):
        pairs = xs[b].shape[0] // SUB

        def place(p, carry, b=b, pairs=pairs):
            piece = xs[b][pl.ds(pl.multiple_of(p * SUB, SUB), SUB), :]
            for s in range(2):
                number = b * 2 * pairs + 2 * p + s
                start = info_ref[0, number]
                group = info_ref[1, number]
                for dest, at in ((real_ref, 2 * s), (imag_ref, 2 * s + 1)):
                    shift = (group * SUB + (LANES - at * SUB)) & (LANES - 1)
                    moved = jnp.where(owner == group, pltpu.roll(piece, shift, 1), 0.0)
                    dest[pl.ds(start, SUB), :] += moved
            return carry

        lax.fori_loop(0, pairs, place, 0)

    step = 16

    def classes(n, carry):
        first = pl.multiple_of(n * step, step)
        real = [real_ref[pl.ds(k * part + first, step), :] for k in range(RADIX)]
        imag = [imag_ref[pl.ds(k * part + first, step), :] for k in range(RADIX)]
        turns = turn_ref[pl.ds(first, step), :]
        for c, (ur, ui) in enumerate(radix_eight(real, imag)):
            cosine = turns[:, c : c + 1]
            sine = turns[:, RADIX + c : RADIX + c + 1]
            vr = ur * cosine - ui * sine
            vi = ur * sine + ui * cosine
            high, low = split(jnp.concatenate([vr, vi], axis=1))
            uh_ref[c, pl.ds(first, step), :] = high
            ul_ref[c, pl.ds(first, step), :] = low
        return carry

    lax.fori_loop(0, part // step, classes, 0)
    dests = out_ref.shape[0]
    half = dests * per_class
    for c in range(RADIX):
        total = dot3(high_ref[...], low_ref[...], uh_ref[c], ul_ref[c])
        real = total[:half, :LANES] - total[half:, LANES:]
        imag = total[:half, LANES:] + total[half:, :LANES]
        for d in range(dests):
            mine = slice(d * per_class, (d + 1) * per_class)
            here = slice(c * per_class, (c + 1) * per_class)
            out_ref[d, here, :LANES] = real[mine]
            out_ref[d, here, LANES:] = imag[mine]


def column_kernel(
    rows_ref, bh_ref, bl_ref, hat_ref, eh_ref, el_ref, th_ref, tl_ref, fh_ref, fl_ref,
    out_ref, qt_ref, qh_ref, ql_ref, corr_ref, v_ref, o_ref, sem,
):
    t = pl.program_id(0)
    tiles = pl.num_programs(0)
    bands = rows_ref.shape[0]
    width = qh_ref.shape[1]
    per_scale = width // NSCALE
    keys = bands * LANES // RADIX

    @pl.when(t == 0)
    def prepare():
        for i in range(bands):
            high, low = split(rows_ref[i])
            product = dot3(high, low, bh_ref[...], bl_ref[...], 0, 0)
            for lane in range(width // LANES):
                cols = slice(lane * LANES, (lane + 1) * LANES)
                qt_ref[0, lane, i * LANES : (i + 1) * LANES, :] = product[:LANES, cols]
                qt_ref[1, lane, i * LANES : (i + 1) * LANES, :] = product[LANES:, cols]
        edge = jnp.zeros((width, LANES), F32)
        for m in range(RADIX):
            parts = []
            for lane in range(width // LANES):
                parts.append(
                    jnp.concatenate(
                        [
                            qt_ref[ri, lane, pl.ds(m, keys, stride=RADIX), :].T
                            for ri in range(2)
                        ],
                        axis=1,
                    )
                )
            q = jnp.concatenate(parts, axis=0)
            high, low = split(q)
            edge = edge + dot3(high, low, eh_ref[m], el_ref[m])
            for scale in range(NSCALE):
                mine = slice(scale * per_scale, (scale + 1) * per_scale)
                qr, qi = q[mine, :keys], q[mine, keys:]
                kr = hat_ref[scale, 0, m : m + 1, :]
                ki = hat_ref[scale, 1, m : m + 1, :]
                high, low = split(
                    jnp.concatenate([qr * kr - qi * ki, qr * ki + qi * kr], axis=1)
                )
                qh_ref[m, mine, :] = high
                ql_ref[m, mine, :] = low
        high, low = split(edge)
        for scale in range(NSCALE):
            mine = slice(scale * per_scale, (scale + 1) * per_scale)
            corr_ref[mine, :] = dot3(high[mine], low[mine], th_ref[scale], tl_ref[scale])

    for m in range(RADIX):
        v_ref[m] = dot3(qh_ref[m], ql_ref[m], fh_ref[0, m], fl_ref[0, m])

    slot = lax.rem(t, 2)

    def copy(which, tile, at):
        return pltpu.make_async_copy(
            o_ref.at[which, at],
            out_ref.at[:, pl.ds(pl.multiple_of((at * tiles + tile) * LANES, LANES), LANES)],
            sem.at[which, at],
        )

    @pl.when(t >= 2)
    def reuse():
        for at in range(RADIX):
            copy(slot, t - 2, at).wait()

    step = 16
    is_first = (t == 0).astype(F32)
    is_last = (t == tiles - 1).astype(F32)

    def combine(n, carry):
        here = pl.ds(pl.multiple_of(n * step, step), step)
        r = [v_ref[m, here, :LANES] for m in range(RADIX)]
        i = [v_ref[m, here, LANES:] if m % 4 else None for m in range(RADIX)]
        s0, s1, s2, s3 = (r[m] + r[m + 4] for m in range(4))
        d0, d1, d3 = r[0] - r[4], r[1] - r[5], r[3] - r[7]
        i1, i3 = i[1] + i[5], i[3] + i[7]
        j1, j2, j3 = i[1] - i[5], i[2] - i[6], i[3] - i[7]
        a, b, c, d = s0 + s2, s0 - s2, s1 + s3, i1 - i3
        e, f = d0 - j2, d0 + j2
        g = ((d1 - j1) - (d3 + j3)) * ROOT_HALF
        h = ((d1 + j1) - (d3 - j3)) * ROOT_HALF
        outs = [
            a + c - is_first * corr_ref[here, :LANES],
            e + g,
            b - d,
            f - h,
            a - c,
            e - g,
            b + d,
            f + h - is_last * corr_ref[here, LANES:],
        ]
        for at in range(RADIX):
            o_ref[slot, at, here, :] = outs[at]
        return carry

    lax.fori_loop(0, width // step, combine, 0)
    for at in range(RADIX):
        copy(slot, t, at).start()

    @pl.when(t == tiles - 1)
    def finish():
        for at in range(RADIX):
            copy(1 - slot, t - 1, at).wait()
            copy(slot, t, at).wait()


def whole(shape):
    return pl.BlockSpec(shape, lambda *_: (0,) * len(shape))


def spread_taps(index, scale_kernels):
    index = jnp.asarray(index, jnp.int32)[None]
    out = jnp.zeros((NSCALE,) + index.shape[1:], F32)
    for u in range(KW):
        out = jnp.where(index == u, scale_kernels[:, u][:, None, None], out)
    return out


def kernel_device(
    vis, vis_pos, vis_w, subgrid_tile, subgrid_group, subgrid_col, grid_kernel, scale_kernels
):
    nr = lax.axis_size("row")
    nc = lax.axis_size("col")
    row, col = lax.axis_index("row"), lax.axis_index("col")
    tile_width = G // nc
    stride = G // nr
    cols_here = G // (nr * nc)
    window = cols_here + 2 * HALO
    per_class = window // RADIX
    part = G // RADIX
    subs = subgrid_col.shape[0]
    width = NSCALE * cols_here

    shifts = [[(i, (i + d) % nc) for i in range(nc)] for d in range(1, nc)]
    info = jnp.stack([subgrid_tile[:, 0] * tile_width + subgrid_col, subgrid_group[:, 0]])
    infos = jnp.concatenate([info] + [lax.ppermute(info, "col", s) for s in shifts], axis=1)

    rotated = jnp.stack(rotated_visibilities(vis, vis_w))
    subgrids = pl.pallas_call(
        subgrid_kernel,
        out_shape=jax.ShapeDtypeStruct((subs // 2 * SUB, LANES), F32),
        compiler_params=pltpu.CompilerParams(vmem_limit_bytes=32 * 2**20),
        name="subgrids",
    )(vis_pos, rotated, grid_kernel.T)
    blocks = [subgrids] + [lax.ppermute(subgrids, "col", s) for s in shifts]

    inner = np.arange(part)
    cosine, sine = turn(
        (stride * np.arange(nr)[:, None] + RADIX * np.arange(per_class)[None, :]).reshape(-1, 1)
        * inner,
        G,
    )
    table_high, table_low = split_table(np.concatenate([cosine, sine], axis=0))
    first_q = np.arange(nc)[:, None, None] * cols_here - HALO
    cosine, sine = turn((first_q + np.arange(RADIX)) * inner[None, :, None], G)
    turns = np.concatenate([cosine, sine], axis=2).astype(np.float32)
    turns = lax.dynamic_index_in_dim(jnp.asarray(turns), col, 0, keepdims=False)
    vmem = pl.BlockSpec(memory_space=pltpu.VMEM)
    rows = pl.pallas_call(
        lambda *refs: row_kernel(*refs, blocks=nc, part=part, per_class=per_class),
        out_shape=jax.ShapeDtypeStruct((nr, window, 2 * LANES), F32),
        in_specs=[pl.BlockSpec(memory_space=pltpu.SMEM)] + [vmem] * (nc + 3),
        out_specs=vmem,
        scratch_shapes=[
            pltpu.VMEM((G, LANES), F32),
            pltpu.VMEM((G, LANES), F32),
            pltpu.VMEM((RADIX, part, 2 * LANES), BF16),
            pltpu.VMEM((RADIX, part, 2 * LANES), BF16),
        ],
        compiler_params=pltpu.CompilerParams(vmem_limit_bytes=48 * 2**20),
        name="rows",
    )(infos, *blocks, turns, jnp.asarray(table_high), jnp.asarray(table_low))

    rows = lax.all_to_all(rows, "row", split_axis=0, concat_axis=0, tiled=True)

    place = (RADIX * np.arange(per_class)[None, :] + np.arange(RADIX)[:, None]).reshape(-1)
    distance = place[:, None] - np.arange(cols_here)[None, :]
    distance = np.where((distance >= 0) & (distance < KW), distance, -1)
    at_q = (row * nc + col) * cols_here - HALO + jnp.asarray(place, jnp.int32)
    inside = ((at_q >= 0) & (at_q < G)).astype(F32) * (1.0 / G)
    across = spread_taps(distance, scale_kernels) * inside[None, :, None]
    across = jnp.concatenate([across[m] for m in range(NSCALE)], axis=1)
    bh, bl = split_outside(across)
    per_band = LANES // RADIX // nc
    keys = (
        np.arange(nr)[:, None, None] * stride
        + np.arange(nc)[None, :, None] * (stride // nc)
        + np.arange(per_band)[None, None, :] * RADIX
    ).reshape(-1)
    k_of = np.arange(RADIX)[:, None] + keys[None, :]
    cosine, sine = turn((np.arange(KW) - HALO)[:, None] * k_of.reshape(1, -1), G)
    hat = jnp.dot(
        scale_kernels,
        jnp.asarray(np.concatenate([cosine, sine], axis=1), F32),
        precision=HIGHEST,
    ).reshape(NSCALE, 2, RADIX, keys.size)
    near = np.arange(-HALO, HALO)
    cosine, sine = turn(k_of[:, :, None] * near, G)
    edge = np.zeros((RADIX, 2 * keys.size, LANES))
    edge[:, : keys.size, : 2 * HALO] = cosine
    edge[:, keys.size :, : 2 * HALO] = -sine
    eh, el = split_table(edge)
    wrap = np.full((LANES, 2 * LANES), -1)
    for e in range(HALO):
        for p in range(e + 1):
            wrap[e, p] = e - p
        for j in range(e, HALO):
            wrap[HALO + e, 2 * LANES - HALO + j] = e + 2 * HALO - j
    th, tl = split_outside(spread_taps(wrap, scale_kernels))
    tiles = part // LANES
    cosine, sine = turn(k_of[:, :, None] * np.arange(part), G)
    table = np.concatenate(
        [
            np.stack([cosine, sine], axis=2),
            np.stack([-sine, cosine], axis=2),
        ],
        axis=1,
    )
    table = table.reshape(RADIX, 2 * keys.size, 2, tiles, LANES).transpose(3, 0, 1, 2, 4)
    fh, fl = split_table(table.reshape(tiles, RADIX, 2 * keys.size, 2 * LANES))
    table_spec = pl.BlockSpec((1, RADIX, 2 * keys.size, 2 * LANES), lambda t: (t, 0, 0, 0))
    operands = (rows, bh, bl, hat, jnp.asarray(eh), jnp.asarray(el), th, tl)
    out = pl.pallas_call(
        column_kernel,
        grid=(tiles,),
        out_shape=jax.ShapeDtypeStruct((width, G), F32),
        in_specs=[whole(o.shape) for o in operands] + [table_spec, table_spec],
        out_specs=pl.BlockSpec(memory_space=pl.ANY),
        scratch_shapes=[
            pltpu.VMEM((2, width // LANES, nr * LANES, LANES), F32),
            pltpu.VMEM((RADIX, width, 2 * keys.size), BF16),
            pltpu.VMEM((RADIX, width, 2 * keys.size), BF16),
            pltpu.VMEM((width, 2 * LANES), F32),
            pltpu.VMEM((RADIX, width, 2 * LANES), F32),
            pltpu.VMEM((2, RADIX, width, LANES), F32),
            pltpu.SemaphoreType.DMA((2, RADIX)),
        ],
        compiler_params=pltpu.CompilerParams(vmem_limit_bytes=56 * 2**20),
        name="columns",
    )(*operands, jnp.asarray(fh), jnp.asarray(fl))
    return out.reshape(NSCALE, cols_here, G)


def solution(mesh):
    nr, nc = mesh.shape["row"], mesh.shape["col"]
    fits = nr == RADIX and nc * SUB == LANES
    return jax.shard_map(
        kernel_device if fits else general_device,
        mesh=mesh,
        in_specs=(
            P(None, ("row", "col")),
            P(None, ("row", "col")),
            P(("row", "col")),
            P(("row", "col"), None),
            P(("row", "col"), None),
            P(("row", "col")),
            P(),
            P(),
        ),
        out_specs=P(None, ("row", "col"), None),
        check_vma=False,
    )
```

```python
import math

import jax
import jax.numpy as jnp
import numpy as np
from jax import lax
from jax.experimental import pallas as pl
from jax.experimental.pallas import tpu as pltpu
from jax.sharding import PartitionSpec as P

G = 8192
SUB = 32
SUP = 8
OVER = 8
VPS = 256
WSTEPS = 1024
KW = 33
NSCALE = 2
HALO = (KW - 1) // 2
RADIX = 8
CLASSES = 16
LANES = 128

HIGHEST = lax.Precision.HIGHEST
F32 = jnp.float32
BF16 = jnp.bfloat16
ROOT_HALF = math.sqrt(0.5)


def with_halo(array, sides, width):
    for axis, dim in sides:
        count, length = (lax.axis_size(axis), array.shape[dim])
        up = [(i, (i + 1) % count) for i in range(count - 1)]
        down = [(j, i) for i, j in up]
        last = lax.slice_in_dim(array, length - width, length, axis=dim)
        initial = lax.slice_in_dim(array, 0, width, axis=dim)
        before = lax.ppermute(last, axis, up)
        after = lax.ppermute(initial, axis, down)
        array = jnp.concatenate([before, array, after], axis=dim)
    return array


def kernel_taps(positions, grid_kernel):
    cell_index = positions // OVER
    fraction = positions % OVER
    onehot = (fraction[:, None] == jnp.arange(OVER, dtype=jnp.int32)[None, :]).astype(
        grid_kernel.dtype
    )
    values = jnp.dot(onehot, grid_kernel, precision=HIGHEST)
    offset = jnp.arange(SUB, dtype=jnp.int32)[None, :] - cell_index[:, None]
    result = jnp.zeros(offset.shape, grid_kernel.dtype)
    for tap_index in range(SUP):
        result = result + jnp.where(offset == tap_index, values[:, tap_index : tap_index + 1], 0.0)
    return result


def rotated_visibilities(vis_block, phase_steps):
    angles = phase_steps.astype(vis_block.dtype) * (2.0 * math.pi / WSTEPS)
    cosine = jnp.cos(angles)
    sine_part = jnp.sin(angles)
    return (
        vis_block[0] * cosine + vis_block[1] * sine_part,
        vis_block[1] * cosine - vis_block[0] * sine_part,
    )


def make_subgrids(vis_block, pos_block, phase_steps, grid_kernel, number):
    along_rows = kernel_taps(pos_block[0], grid_kernel).reshape(number, VPS, SUB)
    along_cols = kernel_taps(pos_block[1], grid_kernel).reshape(number, VPS, SUB)
    rotated_real, rotated_imag = rotated_visibilities(vis_block, phase_steps)
    weighted_real = along_rows * rotated_real.reshape(number, VPS, 1)
    weighted_imag = along_rows * rotated_imag.reshape(number, VPS, 1)
    sub_real = jnp.einsum("sja,sjb->sab", weighted_real, along_cols, precision=HIGHEST)
    sub_imag = jnp.einsum("sja,sjb->sab", weighted_imag, along_cols, precision=HIGHEST)
    return (sub_real, sub_imag)


def dft_table(length):
    positions = jnp.arange(length, dtype=jnp.int32)
    product = positions[:, None] * positions[None, :] % length
    angles = product.astype(jnp.float32) * (2.0 * math.pi / length)
    return (jnp.cos(angles), jnp.sin(angles))


def transform_last(real_part, imag_part, real_only):
    length = real_part.shape[-1]
    factor_one = 2 ** ((length.bit_length() - 1) // 2)
    factor_two = length // factor_one
    leading = real_part.shape[:-1]
    real_part = real_part.reshape(leading + (factor_one, factor_two))
    imag_part = imag_part.reshape(leading + (factor_one, factor_two))
    cos_one, sin_one = dft_table(factor_one)
    section_real = jnp.einsum(
        "...ab,ak->...kb", real_part, cos_one, precision=HIGHEST
    ) - jnp.einsum("...ab,ak->...kb", imag_part, sin_one, precision=HIGHEST)
    section_imag = jnp.einsum(
        "...ab,ak->...kb", real_part, sin_one, precision=HIGHEST
    ) + jnp.einsum("...ab,ak->...kb", imag_part, cos_one, precision=HIGHEST)
    outer_index = (
        jnp.arange(factor_one, dtype=jnp.int32)[:, None]
        * jnp.arange(factor_two, dtype=jnp.int32)[None, :]
        % length
    )
    twiddle = outer_index.astype(jnp.float32) * (2.0 * math.pi / length)
    twiddle_cos = jnp.cos(twiddle)
    twiddle_sin = jnp.sin(twiddle)
    turned_real = section_real * twiddle_cos - section_imag * twiddle_sin
    turned_imag = section_real * twiddle_sin + section_imag * twiddle_cos
    cos_two, sin_two = dft_table(factor_two)
    result_real = jnp.einsum(
        "...kb,bq->...qk", turned_real, cos_two, precision=HIGHEST
    ) - jnp.einsum("...kb,bq->...qk", turned_imag, sin_two, precision=HIGHEST)
    result_real = result_real.reshape(leading + (length,))
    if real_only:
        return result_real
    result_imag = jnp.einsum(
        "...kb,bq->...qk", turned_real, sin_two, precision=HIGHEST
    ) + jnp.einsum("...kb,bq->...qk", turned_imag, cos_two, precision=HIGHEST)
    return (result_real, result_imag.reshape(leading + (length,)))


def band_matrix(kernel_row, height, columns):
    distance = (
        jnp.arange(height, dtype=jnp.int32)[:, None] - jnp.arange(columns, dtype=jnp.int32)[None, :]
    )
    matrix = jnp.zeros((height, columns), jnp.float32)
    for tap_index in range(KW):
        matrix = matrix + jnp.where(distance == tap_index, kernel_row[tap_index], 0.0)
    return matrix


def smooth_along_rows(field, kernel_row):
    height = field.shape[0]
    length = field.shape[1]
    halo_width = (KW - 1) // 2
    block_size = min(128, length)
    blocks = length // block_size
    padded = jnp.pad(field, ((0, 0), (halo_width, block_size - halo_width)))
    framed = padded.reshape(height, blocks + 1, block_size)
    windows = jnp.concatenate([framed[:, :-1, :], framed[:, 1:, : 2 * halo_width]], axis=2)
    matrix = band_matrix(kernel_row, block_size + 2 * halo_width, block_size)
    return jnp.einsum("rni,io->rno", windows, matrix, precision=HIGHEST).reshape(height, length)


def smooth_across(field, kernel_row):
    height = field.shape[0]
    inner_rows = height - (KW - 1)
    matrix = band_matrix(kernel_row, height, inner_rows)
    return jnp.einsum("ry,rx->xy", field, matrix, precision=HIGHEST)


def slot_numbers(bucket_keys, buckets, capacity):
    count = bucket_keys.shape[0]
    index = jnp.arange(count, dtype=jnp.int32)
    same = (bucket_keys[:, None] == bucket_keys[None, :]) & (index[None, :] < index[:, None])
    return bucket_keys * capacity + jnp.sum(same.astype(jnp.int32), axis=1)


def place_blocks(piece_real, piece_imag, owner, start, buckets, width):
    count = piece_real.shape[0]
    piece_rows = piece_real.shape[1] // SUB
    step = math.gcd(count, 32)
    turns = count // step
    piece_real = piece_real.reshape(turns, step, piece_rows, SUB)
    piece_imag = piece_imag.reshape(turns, step, piece_rows, SUB)
    owner = owner.reshape(turns, step)
    start = start.reshape(turns, step)
    column_index = jnp.arange(width, dtype=jnp.int32)
    sub_index = jnp.arange(SUB, dtype=jnp.int32)
    bucket_index = jnp.arange(buckets, dtype=jnp.int32)

    def add_block(carry, block):
        block_real, block_imag, block_owner, block_start = block
        shift = (
            column_index[None, None, :] == block_start[:, None, None] + sub_index[None, :, None]
        ).astype(jnp.float32)
        pick = (block_owner[:, None] == bucket_index[None, :]).astype(jnp.float32)
        moved_real = jnp.einsum("sab,sbc->sac", block_real, shift, precision=HIGHEST)
        moved_imag = jnp.einsum("sab,sbc->sac", block_imag, shift, precision=HIGHEST)
        total_real = carry[0] + jnp.einsum("sg,sac->gac", pick, moved_real, precision=HIGHEST)
        total_imag = carry[1] + jnp.einsum("sg,sac->gac", pick, moved_imag, precision=HIGHEST)
        return ((total_real, total_imag), None)

    empty = jnp.zeros((buckets, piece_rows, width), jnp.float32)
    (placed_real, placed_imag), unused = lax.scan(
        add_block, (empty, empty), (piece_real, piece_imag, owner, start)
    )
    return (placed_real, placed_imag)


def general_device(
    vis, vis_pos, vis_w, subgrid_tile, subgrid_group, subgrid_col, grid_kernel, scale_kernels
):
    row_devices = lax.axis_size("row")
    col_devices = lax.axis_size("col")
    band_rows = G // row_devices
    tile_width = G // col_devices
    group_rows = band_rows // col_devices
    pencil_cols = G // (row_devices * col_devices)
    piece_rows = min(group_rows, SUB)
    pieces = SUB // piece_rows
    subgrids_here = subgrid_col.shape[0]
    batch_size = min(16, subgrids_here)
    batches = subgrids_here // batch_size
    batch_vis = batch_size * VPS

    def grid_batch(step_index):
        start = step_index * batch_vis
        vis_block = lax.dynamic_slice_in_dim(vis, start, batch_vis, 1)
        pos_block = lax.dynamic_slice_in_dim(vis_pos, start, batch_vis, 1)
        phase_block = lax.dynamic_slice_in_dim(vis_w, start, batch_vis, 0)
        sub_real, sub_imag = make_subgrids(
            vis_block, pos_block, phase_block, grid_kernel, batch_size
        )
        return (sub_real.reshape(batch_size, SUB * SUB), sub_imag.reshape(batch_size, SUB * SUB))

    sub_real, sub_imag = lax.map(grid_batch, jnp.arange(batches, dtype=jnp.int32))
    sub_real = sub_real.reshape(subgrids_here, SUB * SUB)
    sub_imag = sub_imag.reshape(subgrids_here, SUB * SUB)
    tile_index = subgrid_tile[:, 0]
    groups = subgrid_group[:, 0]
    groups_used = col_devices - pieces + 1
    most_group = min(subgrids_here, 3 * ((subgrids_here + groups_used - 1) // groups_used) // 2)
    capacity = pieces * most_group
    owners = (groups[:, None] + jnp.arange(pieces, dtype=jnp.int32)[None, :]).reshape(-1)
    starts = jnp.broadcast_to(
        (tile_index * tile_width + subgrid_col)[:, None], (subgrids_here, pieces)
    ).reshape(-1)
    slot_index = slot_numbers(owners, col_devices, capacity)
    piece_real = sub_real.reshape(subgrids_here * pieces, piece_rows * SUB)
    piece_imag = sub_imag.reshape(subgrids_here * pieces, piece_rows * SUB)
    send_real = (
        jnp.zeros((col_devices * capacity, piece_rows * SUB), jnp.float32)
        .at[slot_index]
        .set(piece_real)
    )
    send_imag = (
        jnp.zeros((col_devices * capacity, piece_rows * SUB), jnp.float32)
        .at[slot_index]
        .set(piece_imag)
    )
    send_start = jnp.zeros((col_devices * capacity,), jnp.int32).at[slot_index].set(starts)
    recv_real, recv_imag, recv_start = (
        lax.all_to_all(send_real, "col", split_axis=0, concat_axis=0, tiled=True),
        lax.all_to_all(send_imag, "col", split_axis=0, concat_axis=0, tiled=True),
        lax.all_to_all(send_start, "col", split_axis=0, concat_axis=0, tiled=True),
    )
    placed_real, placed_imag = place_blocks(
        recv_real,
        recv_imag,
        recv_start // tile_width,
        recv_start % tile_width,
        col_devices,
        tile_width,
    )
    widen = ((0, group_rows - piece_rows), (0, 0))
    slab_real = jnp.pad(placed_real.transpose(1, 0, 2).reshape(piece_rows, G), widen)
    slab_imag = jnp.pad(placed_imag.transpose(1, 0, 2).reshape(piece_rows, G), widen)
    rows_real, rows_imag = transform_last(slab_real, slab_imag, False)
    cols_real, cols_imag = (
        lax.all_to_all(
            lax.all_to_all(rows_real, "row", split_axis=1, concat_axis=0, tiled=True),
            "col",
            split_axis=1,
            concat_axis=0,
            tiled=True,
        ),
        lax.all_to_all(
            lax.all_to_all(rows_imag, "row", split_axis=1, concat_axis=0, tiled=True),
            "col",
            split_axis=1,
            concat_axis=0,
            tiled=True,
        ),
    )

    def reorder(field):
        return (
            field.reshape(col_devices, row_devices, group_rows, pencil_cols)
            .transpose(3, 1, 0, 2)
            .reshape(pencil_cols, G)
        )

    image = transform_last(reorder(cols_real), reorder(cols_imag), True) * (1.0 / G)
    halo_width = (KW - 1) // 2
    results = []
    padded = with_halo(image, ((("row", "col"), 0),), halo_width)
    for scale_index in range(NSCALE):
        vertical = smooth_along_rows(padded, scale_kernels[scale_index])
        results.append(smooth_across(vertical, scale_kernels[scale_index]))
    return jnp.stack(results)


def split(value):
    high = value.astype(BF16)
    return high, (value - high.astype(F32)).astype(BF16)


def split_table(table):
    table = np.asarray(table, np.float64)
    high = table.astype(BF16)
    return high, (table - high.astype(np.float64)).astype(BF16)


def turn(steps, length):
    angle = 2.0 * np.pi * (np.asarray(steps, np.int64) % length) / length
    return np.cos(angle), np.sin(angle)


def dot(left, right, left_dim=1, right_dim=0):
    return lax.dot_general(
        left, right, (((left_dim,), (right_dim,)), ((), ())), preferred_element_type=F32
    )


def dot3(left_high, left_low, right_high, right_low, left_dim=1, right_dim=0):
    return (
        dot(left_high, right_high, left_dim, right_dim)
        + dot(left_high, right_low, left_dim, right_dim)
        + dot(left_low, right_high, left_dim, right_dim)
    )


def turned_back(steps):
    quarter = WSTEPS // 4
    turns = (steps + quarter // 2) >> (quarter.bit_length() - 1)
    angle = (steps - turns * quarter).astype(F32) * (2.0 * math.pi / WSTEPS)
    square = angle * angle
    cosine = 1.0 + square * (
        -1 / 2 + square * (1 / 24 + square * (-1 / 720 + square * (1 / 40320 - square / 3628800)))
    )
    sine = angle * (
        1.0 + square * (-1 / 6 + square * (1 / 120 + square * (-1 / 5040 + square / 362880)))
    )
    odd = (turns & 1) == 1
    first, second = jnp.where(odd, sine, cosine), jnp.where(odd, cosine, sine)
    first = jnp.where(((turns + 1) & 2) == 2, -first, first)
    return first, jnp.where((turns & 2) == 2, -second, second)


def subgrid_kernel(pos_ref, vis_ref, phase_ref, taps_ref, info_ref, out_ref):
    span = 2 * VPS
    pairs = vis_ref.shape[1] // span
    diagonal = lax.broadcasted_iota(jnp.int32, (OVER, SUP), 0) == lax.broadcasted_iota(
        jnp.int32, (OVER, SUP), 1
    )
    table = [
        jnp.sum(jnp.where(diagonal, taps_ref[s : s + 1, :], 0.0), axis=1, keepdims=True)
        for s in range(OVER)
    ]

    def taps(position):
        step = position & (OVER - 1)
        cell = position >> (OVER.bit_length() - 1)
        values = jnp.zeros((SUP, span), F32)
        for s in range(OVER):
            values = jnp.where(step == s, table[s], values)
        offset = lax.broadcasted_iota(jnp.int32, (SUB, span), 0) - cell
        result = jnp.zeros((SUB, span), F32)
        for t in range(SUP):
            result = jnp.where(offset == t, values[t : t + 1, :], result)
        return result

    first = lax.broadcasted_iota(jnp.int32, (SUB, LANES), 1) < LANES // 2

    def pair(p, carry):
        here = pl.ds(pl.multiple_of(p * span, span), span)
        along_rows = taps(pos_ref[0:1, here])
        along_cols = taps(pos_ref[1:2, here])
        cosine, sine = turned_back(phase_ref[0:1, here])
        real, imag = vis_ref[0:1, here], vis_ref[1:2, here]
        weighted = jnp.concatenate(
            [
                along_rows * (real * cosine + imag * sine),
                along_rows * (imag * cosine - real * sine),
            ],
            axis=0,
        )
        weighted = jnp.concatenate(split(weighted), axis=0)
        cols = jnp.concatenate(split(along_cols), axis=0)
        sums = []
        for s in range(2):
            part = slice(s * VPS, (s + 1) * VPS)
            product = dot(cols[:, part], weighted[:, part], 1, 1)
            total = product[:SUB] + product[SUB:]
            sums.append(total + pltpu.roll(total, LANES // 2, 1))
        out_ref[pl.ds(pl.multiple_of(p * SUB, SUB), SUB), :] = jnp.where(first, sums[0], sums[1])
        return carry

    lax.fori_loop(0, pairs, pair, 0, unroll=4)
    out_ref[pairs * SUB :, :] = jnp.broadcast_to(
        info_ref[...], (out_ref.shape[0] - pairs * SUB, LANES)
    )


def radix_eight(real, imag):
    def four(r, i):
        a, b = (r[0] + r[2], i[0] + i[2])
        c, d = (r[0] - r[2], i[0] - i[2])
        e, f = (r[1] + r[3], i[1] + i[3])
        g, h = (r[1] - r[3], i[1] - i[3])
        return [(a + e, b + f), (c - h, d + g), (a - e, b - f), (c + h, d - g)]

    low = four(
        [real[n] + real[n + 4] for n in range(4)], [imag[n] + imag[n + 4] for n in range(4)]
    )
    dr = [real[n] - real[n + 4] for n in range(4)]
    di = [imag[n] - imag[n + 4] for n in range(4)]
    high = four(
        [dr[0], (dr[1] - di[1]) * ROOT_HALF, -di[2], (dr[3] + di[3]) * -ROOT_HALF],
        [di[0], (dr[1] + di[1]) * ROOT_HALF, dr[2], (dr[3] - di[3]) * ROOT_HALF],
    )
    return [(low, high)[c % 2][c // 2] for c in range(8)]


def row_kernel(
    info_ref, *refs, blocks, part, per_class
):
    xs = refs[:blocks]
    turn_ref, high_ref, low_ref, out_ref, real_ref, imag_ref, uh_ref, ul_ref = refs[blocks:]
    rows = real_ref.shape[0]
    chunk = 256

    def clear(n, carry):
        here = pl.ds(pl.multiple_of(n * chunk, chunk), chunk)
        real_ref[here, :] = jnp.zeros((chunk, LANES), F32)
        imag_ref[here, :] = jnp.zeros((chunk, LANES), F32)
        return carry

    lax.fori_loop(0, rows // chunk, clear, 0)
    owner = lax.broadcasted_iota(jnp.int32, (SUB, LANES), 1) // SUB
    for b in range(blocks):
        pairs = xs[b].shape[0] // SUB

        def place(p, carry, b=b, pairs=pairs):
            piece = xs[b][pl.ds(pl.multiple_of(p * SUB, SUB), SUB), :]
            for s in range(2):
                start = info_ref[b, 2 * p + s].astype(jnp.int32)
                group = info_ref[b, 2 * pairs + 2 * p + s].astype(jnp.int32)
                for dest, at in ((real_ref, 2 * s), (imag_ref, 2 * s + 1)):
                    shift = (group * SUB + (LANES - at * SUB)) & (LANES - 1)
                    moved = jnp.where(owner == group, pltpu.roll(piece, shift, 1), 0.0)
                    dest[pl.ds(start, SUB), :] += moved
            return carry

        lax.fori_loop(0, pairs, place, 0, unroll=4)

    step = 16

    def classes(n, carry):
        first = pl.multiple_of(n * step, step)
        real = [real_ref[pl.ds(k * part + first, step), :] for k in range(RADIX)]
        imag = [imag_ref[pl.ds(k * part + first, step), :] for k in range(RADIX)]
        turns = turn_ref[pl.ds(first, step), :]
        for c, (ur, ui) in enumerate(radix_eight(real, imag)):
            cosine = turns[:, c : c + 1]
            sine = turns[:, RADIX + c : RADIX + c + 1]
            vr = ur * cosine - ui * sine
            vi = ur * sine + ui * cosine
            high, low = split(jnp.concatenate([vr, vi], axis=1))
            uh_ref[c, pl.ds(first, step), :] = high
            ul_ref[c, pl.ds(first, step), :] = low
        return carry

    lax.fori_loop(0, part // step, classes, 0, unroll=4)
    dests = out_ref.shape[0]
    half = dests * per_class
    for c in range(RADIX):
        total = dot3(high_ref[...], low_ref[...], uh_ref[c], ul_ref[c])
        real = total[:half, :LANES] - total[half:, LANES:]
        imag = total[:half, LANES:] + total[half:, :LANES]
        for d in range(dests):
            mine = slice(d * per_class, (d + 1) * per_class)
            here = slice(c * per_class, (c + 1) * per_class)
            out_ref[d, here, :LANES] = real[mine]
            out_ref[d, here, LANES:] = imag[mine]


def band_kernel(taps_ref, across_ref, wrap_ref, inside_ref, out_ref, th_ref, tl_ref):
    def spread(index, scale):
        out = jnp.zeros(index.shape, F32)
        for u in range(KW):
            out = jnp.where(index == u, taps_ref[scale, u], out)
        return out

    across, wrap = across_ref[...], wrap_ref[...]
    rows = across.shape[0]
    for scale in range(NSCALE):
        cols = slice(scale * across.shape[1], (scale + 1) * across.shape[1])
        high, low = split(spread(across, scale) * inside_ref[...])
        out_ref[:rows, cols] = high
        out_ref[rows : 2 * rows, cols] = high
        out_ref[2 * rows :, cols] = low
        cols = slice(scale * wrap.shape[1], (scale + 1) * wrap.shape[1])
        th_ref[:, cols], tl_ref[:, cols] = split(spread(wrap, scale))


COS1, COS3 = math.cos(math.pi / 8), math.cos(3 * math.pi / 8)


def real_sixteen(h0, h8, x, y):
    a, b = h0 + h8, h0 - h8
    c, d = x[2] + x[6], (x[2] - x[6]) * ROOT_HALF
    even = [a + x[4] + c, b + d, a - x[4], b - d, a + x[4] - c]
    e, f = x[1] - x[7], x[3] - x[5]
    g, h = x[1] + x[7], x[3] + x[5]
    odd = [g + h, e * COS1 + f * COS3, (g - h) * ROOT_HALF, e * COS3 - f * COS1]
    cosines = [even[n] + odd[n] for n in range(4)] + [even[4]]
    cosines += [even[n] - odd[n] for n in (3, 2, 1, 0)]
    k = (y[2] + y[6]) * ROOT_HALF
    even = [None, k + y[4], y[2] - y[6], k - y[4]]
    e, f = y[1] + y[7], y[3] + y[5]
    odd = [
        None,
        e * COS3 + f * COS1,
        (y[1] - y[7] + y[3] - y[5]) * ROOT_HALF,
        e * COS1 - f * COS3,
        y[1] - y[7] - y[3] + y[5],
    ]
    sines = [None] + [even[n] + odd[n] for n in (1, 2, 3)] + [odd[4]]
    sines += [odd[n] - even[n] for n in (3, 2, 1)]
    out = [None] * 16
    out[0], out[8] = cosines[0], cosines[8]
    for n in range(1, 8):
        out[n] = cosines[n] - sines[n]
        out[16 - n] = cosines[n] + sines[n]
    return out


def column_kernel(
    rows_ref, across_ref, hat_ref, eh_ref, el_ref, th_ref, tl_ref, fh_ref, fl_ref,
    out_ref, qt_ref, qh_ref, ql_ref, corr_ref, v_ref, o_ref, sem,
):
    t = pl.program_id(0)
    tiles = pl.num_programs(0)
    bands = rows_ref.shape[0]
    width = qh_ref.shape[1]
    per_scale = width // NSCALE
    keys = LANES // 2

    @pl.when(t == 0)
    def prepare():
        for i in range(bands):
            high, low = split(rows_ref[i])
            product = dot(jnp.concatenate([high, low, high], axis=0), across_ref[...], 0, 0)
            for lane in range(width // LANES):
                cols = slice(lane * LANES, (lane + 1) * LANES)
                qt_ref[0, lane, i * LANES : (i + 1) * LANES, :] = product[:LANES, cols]
                qt_ref[1, lane, i * LANES : (i + 1) * LANES, :] = product[LANES:, cols]
        edge = jnp.zeros((width, LANES), F32)
        half = CLASSES // 2
        for slot in range(half):
            halves = []
            for m in (slot, CLASSES - slot if slot else half):
                parts = []
                for lane in range(width // LANES):
                    here = pl.ds(m, keys, stride=CLASSES)
                    pair = [qt_ref[ri, lane, here, :] for ri in range(2)]
                    parts.append(jnp.concatenate(pair, axis=0).T)
                halves.append(jnp.concatenate(parts, axis=0))
            high, low = split(jnp.concatenate(halves, axis=1))
            edge = edge + dot3(high, low, eh_ref[slot], el_ref[slot])
            for at, m in enumerate((slot, CLASSES - slot if slot else half)):
                q = halves[at]
                turned = pltpu.roll(q, keys, 1)
                lanes = slice(at * LANES, (at + 1) * LANES)
                for scale in range(NSCALE):
                    mine = slice(scale * per_scale, (scale + 1) * per_scale)
                    high, low = split(
                        q[mine] * hat_ref[scale, 0, m : m + 1, :]
                        + turned[mine] * hat_ref[scale, 1, m : m + 1, :]
                    )
                    qh_ref[slot, mine, lanes] = high
                    ql_ref[slot, mine, lanes] = low
        high, low = split(edge)
        for scale in range(NSCALE):
            mine = slice(scale * per_scale, (scale + 1) * per_scale)
            cols = slice(scale * 2 * LANES, (scale + 1) * 2 * LANES)
            corr_ref[mine, :] = dot3(high[mine], low[mine], th_ref[:, cols], tl_ref[:, cols])

    for m in range(CLASSES // 2):
        v_ref[m] = dot3(qh_ref[m], ql_ref[m], fh_ref[0, m], fl_ref[0, m])

    slot = lax.rem(t, 2)

    def copy(which, tile, at):
        return pltpu.make_async_copy(
            o_ref.at[which, at],
            out_ref.at[:, pl.ds(pl.multiple_of((at * tiles + tile) * LANES, LANES), LANES)],
            sem.at[which, at],
        )

    @pl.when(t >= 2)
    def reuse():
        for at in range(CLASSES):
            copy(slot, t - 2, at).wait()

    step = 8
    is_first = (t == 0).astype(F32)
    is_last = (t == tiles - 1).astype(F32)

    def combine(n, carry):
        here = pl.ds(pl.multiple_of(n * step, step), step)
        x = [v_ref[m, here, :LANES] for m in range(CLASSES // 2)]
        y = [v_ref[m, here, LANES:] for m in range(CLASSES // 2)]
        outs = real_sixteen(x[0], y[0], x, y)
        outs[0] = outs[0] - is_first * corr_ref[here, :LANES]
        outs[-1] = outs[-1] - is_last * corr_ref[here, LANES:]
        for at in range(CLASSES):
            o_ref[slot, at, here, :] = outs[at]
        return carry

    lax.fori_loop(0, width // step, combine, 0, unroll=4)
    for at in range(CLASSES):
        copy(slot, t, at).start()

    @pl.when(t == tiles - 1)
    def finish():
        for at in range(CLASSES):
            copy(1 - slot, t - 1, at).wait()
            copy(slot, t, at).wait()


def whole(shape):
    return pl.BlockSpec(shape, lambda *_: (0,) * len(shape))


def kernel_device(
    vis, vis_pos, vis_w, subgrid_tile, subgrid_group, subgrid_col, grid_kernel, scale_kernels
):
    nr = lax.axis_size("row")
    nc = lax.axis_size("col")
    row, col = lax.axis_index("row"), lax.axis_index("col")
    tile_width = G // nc
    stride = G // nr
    cols_here = G // (nr * nc)
    window = cols_here + 2 * HALO
    per_class = window // RADIX
    part = G // RADIX
    subs = subgrid_col.shape[0]
    width = NSCALE * cols_here

    corner = subgrid_tile[:, 0] * tile_width + subgrid_col
    info = jnp.concatenate([corner, subgrid_group[:, 0]]).astype(F32)
    info = jnp.pad(info, (0, LANES - info.shape[0]))[None]
    rows_of_pairs = subs // 2 * SUB
    subgrids = pl.pallas_call(
        subgrid_kernel,
        out_shape=jax.ShapeDtypeStruct((rows_of_pairs + 8, LANES), F32),
        compiler_params=pltpu.CompilerParams(vmem_limit_bytes=32 * 2**20),
        name="subgrids",
    )(vis_pos, vis, vis_w[None], grid_kernel, info)
    shifts = [[(i, (i + d) % nc) for i in range(nc)] for d in range(1, nc)]
    blocks = [subgrids] + [lax.ppermute(subgrids, "col", s) for s in shifts]
    infos = jnp.concatenate([b[rows_of_pairs : rows_of_pairs + 1] for b in blocks], axis=0)

    inner = np.arange(part)
    cosine, sine = turn(
        (stride * np.arange(nr)[:, None] + RADIX * np.arange(per_class)[None, :]).reshape(-1, 1)
        * inner,
        G,
    )
    table_high, table_low = split_table(np.concatenate([cosine, sine], axis=0))
    first_q = np.arange(nc)[:, None, None] * cols_here - HALO
    cosine, sine = turn((first_q + np.arange(RADIX)) * inner[None, :, None], G)
    turns = np.concatenate([cosine, sine], axis=2).astype(np.float32)
    turns = lax.dynamic_index_in_dim(jnp.asarray(turns), col, 0, keepdims=False)
    vmem = pl.BlockSpec(memory_space=pltpu.VMEM)
    rows = pl.pallas_call(
        lambda *refs: row_kernel(*refs, blocks=nc, part=part, per_class=per_class),
        out_shape=jax.ShapeDtypeStruct((nr, window, 2 * LANES), F32),
        in_specs=[pl.BlockSpec(memory_space=pltpu.SMEM)] + [vmem] * (nc + 3),
        out_specs=vmem,
        scratch_shapes=[
            pltpu.VMEM((G, LANES), F32),
            pltpu.VMEM((G, LANES), F32),
            pltpu.VMEM((RADIX, part, 2 * LANES), BF16),
            pltpu.VMEM((RADIX, part, 2 * LANES), BF16),
        ],
        compiler_params=pltpu.CompilerParams(vmem_limit_bytes=48 * 2**20),
        name="rows",
    )(infos, *blocks, turns, jnp.asarray(table_high), jnp.asarray(table_low))

    rows = lax.all_to_all(rows, "row", split_axis=0, concat_axis=0, tiled=True)

    place = (RADIX * np.arange(per_class)[None, :] + np.arange(RADIX)[:, None]).reshape(-1)
    distance = place[:, None] - np.arange(cols_here)[None, :]
    distance = np.where((distance >= 0) & (distance < KW), distance, -1)
    at_q = (row * nc + col) * cols_here - HALO + jnp.asarray(place, jnp.int32)
    inside = ((at_q >= 0) & (at_q < G)).astype(F32) * (1.0 / G)
    wrap = np.full((LANES, 2 * LANES), -1)
    for e in range(HALO):
        for p in range(e + 1):
            wrap[e, p] = e - p
        for j in range(e, HALO):
            wrap[HALO + e, 2 * LANES - HALO + j] = e + 2 * HALO - j
    across, th, tl = pl.pallas_call(
        band_kernel,
        out_shape=[jax.ShapeDtypeStruct((3 * window, width), BF16)]
        + [jax.ShapeDtypeStruct((LANES, NSCALE * 2 * LANES), BF16)] * 2,
        in_specs=[pl.BlockSpec(memory_space=pltpu.SMEM)] + [vmem] * 3,
        out_specs=[vmem] * 3,
        compiler_params=pltpu.CompilerParams(vmem_limit_bytes=32 * 2**20),
        name="bands",
    )(
        scale_kernels,
        jnp.asarray(distance, jnp.int32),
        jnp.asarray(wrap, jnp.int32),
        inside[:, None],
    )
    per_band = LANES // CLASSES // nc
    keys = (
        np.arange(nr)[:, None, None] * stride
        + np.arange(nc)[None, :, None] * (stride // nc)
        + np.arange(per_band)[None, None, :] * CLASSES
    ).reshape(-1)
    k_of = np.arange(CLASSES)[:, None] + keys[None, :]
    cosine, sine = turn((np.arange(KW) - HALO)[:, None, None] * k_of, G)
    hat_table = np.stack(
        [
            np.concatenate([cosine, cosine], axis=2),
            np.concatenate([-sine, sine], axis=2),
        ],
        axis=1,
    )
    hat = jnp.dot(
        scale_kernels, jnp.asarray(hat_table.reshape(KW, -1), F32), precision=HIGHEST
    ).reshape(NSCALE, 2, CLASSES, 2 * keys.size)
    near = np.arange(-HALO, HALO)
    cosine, sine = turn(k_of[:, :, None] * near, G)
    edge = np.zeros((CLASSES, 2 * keys.size, LANES))
    edge[:, : keys.size, : 2 * HALO] = cosine
    edge[:, keys.size :, : 2 * HALO] = -sine
    half = CLASSES // 2
    others = [CLASSES - m if m else half for m in range(half)]
    eh, el = split_table(np.concatenate([edge[:half], edge[others]], axis=1))
    span = G // CLASSES
    tiles = span // LANES
    cosine, sine = turn(k_of[:, :, None] * np.arange(span), G)
    real = np.concatenate([cosine, -sine], axis=1)
    imag = np.concatenate([sine, cosine], axis=1)
    none = np.zeros_like(real[0])
    table = [np.block([[real[0], none], [none, real[half]]])]
    for m in range(1, half):
        other = CLASSES - m
        table.append(np.block([[real[m], imag[m]], [real[other], -imag[other]]]))
    table = np.stack(table).reshape(half, 4 * keys.size, 2, tiles, LANES)
    table = table.transpose(3, 0, 1, 2, 4).reshape(tiles, half, 4 * keys.size, 2 * LANES)
    fh, fl = split_table(table)
    table_spec = pl.BlockSpec((1,) + table.shape[1:], lambda t: (t, 0, 0, 0))
    operands = (rows, across, hat, jnp.asarray(eh), jnp.asarray(el), th, tl)
    out = pl.pallas_call(
        column_kernel,
        grid=(tiles,),
        out_shape=jax.ShapeDtypeStruct((width, G), F32),
        in_specs=[whole(o.shape) for o in operands] + [table_spec, table_spec],
        out_specs=pl.BlockSpec(memory_space=pl.ANY),
        scratch_shapes=[
            pltpu.VMEM((2, width // LANES, nr * LANES, LANES), F32),
            pltpu.VMEM((half, width, 4 * keys.size), BF16),
            pltpu.VMEM((half, width, 4 * keys.size), BF16),
            pltpu.VMEM((width, 2 * LANES), F32),
            pltpu.VMEM((half, width, 2 * LANES), F32),
            pltpu.VMEM((2, CLASSES, width, LANES), F32),
            pltpu.SemaphoreType.DMA((2, CLASSES)),
        ],
        compiler_params=pltpu.CompilerParams(vmem_limit_bytes=56 * 2**20),
        name="columns",
    )(*operands, jnp.asarray(fh), jnp.asarray(fl))
    return out.reshape(NSCALE, cols_here, G)


def solution(mesh):
    nr, nc = mesh.shape["row"], mesh.shape["col"]
    fits = nr == RADIX and nc * SUB == LANES
    return jax.shard_map(
        kernel_device if fits else general_device,
        mesh=mesh,
        in_specs=(
            P(None, ("row", "col")),
            P(None, ("row", "col")),
            P(("row", "col")),
            P(("row", "col"), None),
            P(("row", "col"), None),
            P(("row", "col")),
            P(),
            P(),
        ),
        out_specs=P(None, ("row", "col"), None),
        check_vma=False,
    )
```

```python
import math

import jax
import jax.numpy as jnp
import numpy as np
from jax import lax
from jax.experimental import pallas as pl
from jax.experimental.pallas import tpu as pltpu
from jax.sharding import PartitionSpec as P

G = 8192
SUB = 32
SUP = 8
OVER = 8
VPS = 256
WSTEPS = 1024
KW = 33
NSCALE = 2
HALO = (KW - 1) // 2
RADIX = 8
CLASSES = 16
LANES = 128

HIGHEST = lax.Precision.HIGHEST
F32 = jnp.float32
BF16 = jnp.bfloat16
ROOT_HALF = math.sqrt(0.5)


def with_halo(array, sides, width):
    for axis, dim in sides:
        count, length = (lax.axis_size(axis), array.shape[dim])
        up = [(i, (i + 1) % count) for i in range(count - 1)]
        down = [(j, i) for i, j in up]
        last = lax.slice_in_dim(array, length - width, length, axis=dim)
        initial = lax.slice_in_dim(array, 0, width, axis=dim)
        before = lax.ppermute(last, axis, up)
        after = lax.ppermute(initial, axis, down)
        array = jnp.concatenate([before, array, after], axis=dim)
    return array


def kernel_taps(positions, grid_kernel):
    cell_index = positions // OVER
    fraction = positions % OVER
    onehot = (fraction[:, None] == jnp.arange(OVER, dtype=jnp.int32)[None, :]).astype(
        grid_kernel.dtype
    )
    values = jnp.dot(onehot, grid_kernel, precision=HIGHEST)
    offset = jnp.arange(SUB, dtype=jnp.int32)[None, :] - cell_index[:, None]
    result = jnp.zeros(offset.shape, grid_kernel.dtype)
    for tap_index in range(SUP):
        result = result + jnp.where(offset == tap_index, values[:, tap_index : tap_index + 1], 0.0)
    return result


def rotated_visibilities(vis_block, phase_steps):
    angles = phase_steps.astype(vis_block.dtype) * (2.0 * math.pi / WSTEPS)
    cosine = jnp.cos(angles)
    sine_part = jnp.sin(angles)
    return (
        vis_block[0] * cosine + vis_block[1] * sine_part,
        vis_block[1] * cosine - vis_block[0] * sine_part,
    )


def make_subgrids(vis_block, pos_block, phase_steps, grid_kernel, number):
    along_rows = kernel_taps(pos_block[0], grid_kernel).reshape(number, VPS, SUB)
    along_cols = kernel_taps(pos_block[1], grid_kernel).reshape(number, VPS, SUB)
    rotated_real, rotated_imag = rotated_visibilities(vis_block, phase_steps)
    weighted_real = along_rows * rotated_real.reshape(number, VPS, 1)
    weighted_imag = along_rows * rotated_imag.reshape(number, VPS, 1)
    sub_real = jnp.einsum("sja,sjb->sab", weighted_real, along_cols, precision=HIGHEST)
    sub_imag = jnp.einsum("sja,sjb->sab", weighted_imag, along_cols, precision=HIGHEST)
    return (sub_real, sub_imag)


def dft_table(length):
    positions = jnp.arange(length, dtype=jnp.int32)
    product = positions[:, None] * positions[None, :] % length
    angles = product.astype(jnp.float32) * (2.0 * math.pi / length)
    return (jnp.cos(angles), jnp.sin(angles))


def transform_last(real_part, imag_part, real_only):
    length = real_part.shape[-1]
    factor_one = 2 ** ((length.bit_length() - 1) // 2)
    factor_two = length // factor_one
    leading = real_part.shape[:-1]
    real_part = real_part.reshape(leading + (factor_one, factor_two))
    imag_part = imag_part.reshape(leading + (factor_one, factor_two))
    cos_one, sin_one = dft_table(factor_one)
    section_real = jnp.einsum(
        "...ab,ak->...kb", real_part, cos_one, precision=HIGHEST
    ) - jnp.einsum("...ab,ak->...kb", imag_part, sin_one, precision=HIGHEST)
    section_imag = jnp.einsum(
        "...ab,ak->...kb", real_part, sin_one, precision=HIGHEST
    ) + jnp.einsum("...ab,ak->...kb", imag_part, cos_one, precision=HIGHEST)
    outer_index = (
        jnp.arange(factor_one, dtype=jnp.int32)[:, None]
        * jnp.arange(factor_two, dtype=jnp.int32)[None, :]
        % length
    )
    twiddle = outer_index.astype(jnp.float32) * (2.0 * math.pi / length)
    twiddle_cos = jnp.cos(twiddle)
    twiddle_sin = jnp.sin(twiddle)
    turned_real = section_real * twiddle_cos - section_imag * twiddle_sin
    turned_imag = section_real * twiddle_sin + section_imag * twiddle_cos
    cos_two, sin_two = dft_table(factor_two)
    result_real = jnp.einsum(
        "...kb,bq->...qk", turned_real, cos_two, precision=HIGHEST
    ) - jnp.einsum("...kb,bq->...qk", turned_imag, sin_two, precision=HIGHEST)
    result_real = result_real.reshape(leading + (length,))
    if real_only:
        return result_real
    result_imag = jnp.einsum(
        "...kb,bq->...qk", turned_real, sin_two, precision=HIGHEST
    ) + jnp.einsum("...kb,bq->...qk", turned_imag, cos_two, precision=HIGHEST)
    return (result_real, result_imag.reshape(leading + (length,)))


def band_matrix(kernel_row, height, columns):
    distance = (
        jnp.arange(height, dtype=jnp.int32)[:, None] - jnp.arange(columns, dtype=jnp.int32)[None, :]
    )
    matrix = jnp.zeros((height, columns), jnp.float32)
    for tap_index in range(KW):
        matrix = matrix + jnp.where(distance == tap_index, kernel_row[tap_index], 0.0)
    return matrix


def smooth_along_rows(field, kernel_row):
    height = field.shape[0]
    length = field.shape[1]
    halo_width = (KW - 1) // 2
    block_size = min(128, length)
    blocks = length // block_size
    padded = jnp.pad(field, ((0, 0), (halo_width, block_size - halo_width)))
    framed = padded.reshape(height, blocks + 1, block_size)
    windows = jnp.concatenate([framed[:, :-1, :], framed[:, 1:, : 2 * halo_width]], axis=2)
    matrix = band_matrix(kernel_row, block_size + 2 * halo_width, block_size)
    return jnp.einsum("rni,io->rno", windows, matrix, precision=HIGHEST).reshape(height, length)


def smooth_across(field, kernel_row):
    height = field.shape[0]
    inner_rows = height - (KW - 1)
    matrix = band_matrix(kernel_row, height, inner_rows)
    return jnp.einsum("ry,rx->xy", field, matrix, precision=HIGHEST)


def slot_numbers(bucket_keys, buckets, capacity):
    count = bucket_keys.shape[0]
    index = jnp.arange(count, dtype=jnp.int32)
    same = (bucket_keys[:, None] == bucket_keys[None, :]) & (index[None, :] < index[:, None])
    return bucket_keys * capacity + jnp.sum(same.astype(jnp.int32), axis=1)


def place_blocks(piece_real, piece_imag, owner, start, buckets, width):
    count = piece_real.shape[0]
    piece_rows = piece_real.shape[1] // SUB
    step = math.gcd(count, 32)
    turns = count // step
    piece_real = piece_real.reshape(turns, step, piece_rows, SUB)
    piece_imag = piece_imag.reshape(turns, step, piece_rows, SUB)
    owner = owner.reshape(turns, step)
    start = start.reshape(turns, step)
    column_index = jnp.arange(width, dtype=jnp.int32)
    sub_index = jnp.arange(SUB, dtype=jnp.int32)
    bucket_index = jnp.arange(buckets, dtype=jnp.int32)

    def add_block(carry, block):
        block_real, block_imag, block_owner, block_start = block
        shift = (
            column_index[None, None, :] == block_start[:, None, None] + sub_index[None, :, None]
        ).astype(jnp.float32)
        pick = (block_owner[:, None] == bucket_index[None, :]).astype(jnp.float32)
        moved_real = jnp.einsum("sab,sbc->sac", block_real, shift, precision=HIGHEST)
        moved_imag = jnp.einsum("sab,sbc->sac", block_imag, shift, precision=HIGHEST)
        total_real = carry[0] + jnp.einsum("sg,sac->gac", pick, moved_real, precision=HIGHEST)
        total_imag = carry[1] + jnp.einsum("sg,sac->gac", pick, moved_imag, precision=HIGHEST)
        return ((total_real, total_imag), None)

    empty = jnp.zeros((buckets, piece_rows, width), jnp.float32)
    (placed_real, placed_imag), unused = lax.scan(
        add_block, (empty, empty), (piece_real, piece_imag, owner, start)
    )
    return (placed_real, placed_imag)


def general_device(
    vis, vis_pos, vis_w, subgrid_tile, subgrid_group, subgrid_col, grid_kernel, scale_kernels
):
    row_devices = lax.axis_size("row")
    col_devices = lax.axis_size("col")
    band_rows = G // row_devices
    tile_width = G // col_devices
    group_rows = band_rows // col_devices
    pencil_cols = G // (row_devices * col_devices)
    piece_rows = min(group_rows, SUB)
    pieces = SUB // piece_rows
    subgrids_here = subgrid_col.shape[0]
    batch_size = min(16, subgrids_here)
    batches = subgrids_here // batch_size
    batch_vis = batch_size * VPS

    def grid_batch(step_index):
        start = step_index * batch_vis
        vis_block = lax.dynamic_slice_in_dim(vis, start, batch_vis, 1)
        pos_block = lax.dynamic_slice_in_dim(vis_pos, start, batch_vis, 1)
        phase_block = lax.dynamic_slice_in_dim(vis_w, start, batch_vis, 0)
        sub_real, sub_imag = make_subgrids(
            vis_block, pos_block, phase_block, grid_kernel, batch_size
        )
        return (sub_real.reshape(batch_size, SUB * SUB), sub_imag.reshape(batch_size, SUB * SUB))

    sub_real, sub_imag = lax.map(grid_batch, jnp.arange(batches, dtype=jnp.int32))
    sub_real = sub_real.reshape(subgrids_here, SUB * SUB)
    sub_imag = sub_imag.reshape(subgrids_here, SUB * SUB)
    tile_index = subgrid_tile[:, 0]
    groups = subgrid_group[:, 0]
    groups_used = col_devices - pieces + 1
    most_group = min(subgrids_here, 3 * ((subgrids_here + groups_used - 1) // groups_used) // 2)
    capacity = pieces * most_group
    owners = (groups[:, None] + jnp.arange(pieces, dtype=jnp.int32)[None, :]).reshape(-1)
    starts = jnp.broadcast_to(
        (tile_index * tile_width + subgrid_col)[:, None], (subgrids_here, pieces)
    ).reshape(-1)
    slot_index = slot_numbers(owners, col_devices, capacity)
    piece_real = sub_real.reshape(subgrids_here * pieces, piece_rows * SUB)
    piece_imag = sub_imag.reshape(subgrids_here * pieces, piece_rows * SUB)
    send_real = (
        jnp.zeros((col_devices * capacity, piece_rows * SUB), jnp.float32)
        .at[slot_index]
        .set(piece_real)
    )
    send_imag = (
        jnp.zeros((col_devices * capacity, piece_rows * SUB), jnp.float32)
        .at[slot_index]
        .set(piece_imag)
    )
    send_start = jnp.zeros((col_devices * capacity,), jnp.int32).at[slot_index].set(starts)
    recv_real, recv_imag, recv_start = (
        lax.all_to_all(send_real, "col", split_axis=0, concat_axis=0, tiled=True),
        lax.all_to_all(send_imag, "col", split_axis=0, concat_axis=0, tiled=True),
        lax.all_to_all(send_start, "col", split_axis=0, concat_axis=0, tiled=True),
    )
    placed_real, placed_imag = place_blocks(
        recv_real,
        recv_imag,
        recv_start // tile_width,
        recv_start % tile_width,
        col_devices,
        tile_width,
    )
    widen = ((0, group_rows - piece_rows), (0, 0))
    slab_real = jnp.pad(placed_real.transpose(1, 0, 2).reshape(piece_rows, G), widen)
    slab_imag = jnp.pad(placed_imag.transpose(1, 0, 2).reshape(piece_rows, G), widen)
    rows_real, rows_imag = transform_last(slab_real, slab_imag, False)
    cols_real, cols_imag = (
        lax.all_to_all(
            lax.all_to_all(rows_real, "row", split_axis=1, concat_axis=0, tiled=True),
            "col",
            split_axis=1,
            concat_axis=0,
            tiled=True,
        ),
        lax.all_to_all(
            lax.all_to_all(rows_imag, "row", split_axis=1, concat_axis=0, tiled=True),
            "col",
            split_axis=1,
            concat_axis=0,
            tiled=True,
        ),
    )

    def reorder(field):
        return (
            field.reshape(col_devices, row_devices, group_rows, pencil_cols)
            .transpose(3, 1, 0, 2)
            .reshape(pencil_cols, G)
        )

    image = transform_last(reorder(cols_real), reorder(cols_imag), True) * (1.0 / G)
    halo_width = (KW - 1) // 2
    results = []
    padded = with_halo(image, ((("row", "col"), 0),), halo_width)
    for scale_index in range(NSCALE):
        vertical = smooth_along_rows(padded, scale_kernels[scale_index])
        results.append(smooth_across(vertical, scale_kernels[scale_index]))
    return jnp.stack(results)


def split(value):
    high = value.astype(BF16)
    return high, (value - high.astype(F32)).astype(BF16)


def split_table(table):
    table = np.asarray(table, np.float64)
    high = table.astype(BF16)
    return high, (table - high.astype(np.float64)).astype(BF16)


def turn(steps, length):
    angle = 2.0 * np.pi * (np.asarray(steps, np.int64) % length) / length
    return np.cos(angle), np.sin(angle)


def dot(left, right, left_dim=1, right_dim=0):
    return lax.dot_general(
        left, right, (((left_dim,), (right_dim,)), ((), ())), preferred_element_type=F32
    )


def dot3(left_high, left_low, right_high, right_low, left_dim=1, right_dim=0):
    return (
        dot(left_high, right_high, left_dim, right_dim)
        + dot(left_high, right_low, left_dim, right_dim)
        + dot(left_low, right_high, left_dim, right_dim)
    )


def subgrid_kernel(packed_ref, taps_ref, out_ref):
    span = 2 * VPS
    pairs = out_ref.shape[0] // SUB
    diagonal = lax.broadcasted_iota(jnp.int32, (OVER, SUP), 0) == lax.broadcasted_iota(
        jnp.int32, (OVER, SUP), 1
    )
    table = [
        jnp.sum(jnp.where(diagonal, taps_ref[s : s + 1, :], 0.0), axis=1, keepdims=True)
        for s in range(OVER)
    ]

    def taps(position):
        step = position & (OVER - 1)
        cell = position >> (OVER.bit_length() - 1)
        values = jnp.zeros((SUP, span), F32)
        for s in range(OVER):
            values = jnp.where(step == s, table[s], values)
        offset = lax.broadcasted_iota(jnp.int32, (SUB, span), 0) - cell
        result = jnp.zeros((SUB, span), F32)
        for t in range(SUP):
            result = jnp.where(offset == t, values[t : t + 1, :], result)
        return result

    first = lax.broadcasted_iota(jnp.int32, (SUB, LANES), 1) < LANES // 2

    def pair(p, carry):
        here = pl.ds(pl.multiple_of(p * span, span), span)
        along_rows = taps(packed_ref[2:3, here].astype(jnp.int32))
        along_cols = taps(packed_ref[3:4, here].astype(jnp.int32))
        weighted = jnp.concatenate(
            [along_rows * packed_ref[0:1, here], along_rows * packed_ref[1:2, here]], axis=0
        )
        weighted = jnp.concatenate(split(weighted), axis=0)
        cols = jnp.concatenate(split(along_cols), axis=0)
        sums = []
        for s in range(2):
            part = slice(s * VPS, (s + 1) * VPS)
            product = dot(cols[:, part], weighted[:, part], 1, 1)
            total = product[:SUB] + product[SUB:]
            sums.append(total + pltpu.roll(total, LANES // 2, 1))
        out_ref[pl.ds(pl.multiple_of(p * SUB, SUB), SUB), :] = jnp.where(first, sums[0], sums[1])
        return carry

    lax.fori_loop(0, pairs, pair, 0, unroll=8)


def radix_eight(real, imag):
    def four(r, i):
        a, b = (r[0] + r[2], i[0] + i[2])
        c, d = (r[0] - r[2], i[0] - i[2])
        e, f = (r[1] + r[3], i[1] + i[3])
        g, h = (r[1] - r[3], i[1] - i[3])
        return [(a + e, b + f), (c - h, d + g), (a - e, b - f), (c + h, d - g)]

    low = four(
        [real[n] + real[n + 4] for n in range(4)], [imag[n] + imag[n + 4] for n in range(4)]
    )
    dr = [real[n] - real[n + 4] for n in range(4)]
    di = [imag[n] - imag[n + 4] for n in range(4)]
    high = four(
        [dr[0], (dr[1] - di[1]) * ROOT_HALF, -di[2], (dr[3] + di[3]) * -ROOT_HALF],
        [di[0], (dr[1] + di[1]) * ROOT_HALF, dr[2], (dr[3] - di[3]) * ROOT_HALF],
    )
    return [(low, high)[c % 2][c // 2] for c in range(8)]


def row_kernel(info_ref, *refs, blocks, part, per_class, tile_width):
    xs = refs[:blocks]
    turn_ref, tables_ref, out_ref, real_ref, imag_ref, uh_ref, ul_ref, both_ref, sem = refs[blocks:]
    fetch = pltpu.make_async_copy(tables_ref, both_ref, sem)
    fetch.start()
    rows = real_ref.shape[0]
    chunk = 256

    def clear(n, carry):
        here = pl.ds(pl.multiple_of(n * chunk, chunk), chunk)
        real_ref[here, :] = jnp.zeros((chunk, LANES), F32)
        imag_ref[here, :] = jnp.zeros((chunk, LANES), F32)
        return carry

    lax.fori_loop(0, rows // chunk, clear, 0)
    owner = lax.broadcasted_iota(jnp.int32, (SUB, LANES), 1) // SUB
    for b in range(blocks):
        pairs = xs[b].shape[0] // SUB

        def place(p, carry, b=b, pairs=pairs):
            piece = xs[b][pl.ds(pl.multiple_of(p * SUB, SUB), SUB), :]
            for s in range(2):
                number = 2 * p + s
                tile, group, start = (
                    info_ref[b, n * 2 * pairs + number].astype(jnp.int32) for n in range(3)
                )
                start = tile * tile_width + start
                for dest, at in ((real_ref, 2 * s), (imag_ref, 2 * s + 1)):
                    shift = (group * SUB + (LANES - at * SUB)) & (LANES - 1)
                    moved = jnp.where(owner == group, pltpu.roll(piece, shift, 1), 0.0)
                    dest[pl.ds(start, SUB), :] += moved
            return carry

        lax.fori_loop(0, pairs, place, 0, unroll=4)

    step = 16

    def classes(n, carry):
        first = pl.multiple_of(n * step, step)
        real = [real_ref[pl.ds(k * part + first, step), :] for k in range(RADIX)]
        imag = [imag_ref[pl.ds(k * part + first, step), :] for k in range(RADIX)]
        turns = turn_ref[pl.ds(first, step), :]
        for c, (ur, ui) in enumerate(radix_eight(real, imag)):
            cosine = turns[:, c : c + 1]
            sine = turns[:, RADIX + c : RADIX + c + 1]
            vr = ur * cosine - ui * sine
            vi = ur * sine + ui * cosine
            high, low = split(jnp.concatenate([vr, vi], axis=1))
            uh_ref[c, pl.ds(first, step), :] = high
            ul_ref[c, pl.ds(first, step), :] = low
        return carry

    lax.fori_loop(0, part // step, classes, 0, unroll=4)
    dests = out_ref.shape[0]
    half = dests * per_class
    fetch.wait()
    for c in range(RADIX):
        total = dot3(both_ref[0], both_ref[1], uh_ref[c], ul_ref[c])
        real = total[:half, :LANES] - total[half:, LANES:]
        imag = total[:half, LANES:] + total[half:, :LANES]
        for d in range(dests):
            mine = slice(d * per_class, (d + 1) * per_class)
            here = slice(c * per_class, (c + 1) * per_class)
            out_ref[d, here, :LANES] = real[mine]
            out_ref[d, here, LANES:] = imag[mine]


def band_kernel(taps_ref, across_ref, wrap_ref, inside_ref, out_ref, th_ref, tl_ref):
    def spread(index, scale):
        out = jnp.zeros(index.shape, F32)
        for u in range(KW):
            out = jnp.where(index == u, taps_ref[scale, u], out)
        return out

    across, wrap = across_ref[...], wrap_ref[...]
    rows = across.shape[0]
    for scale in range(NSCALE):
        cols = slice(scale * across.shape[1], (scale + 1) * across.shape[1])
        high, low = split(spread(across, scale) * inside_ref[...])
        out_ref[:rows, cols] = high
        out_ref[rows : 2 * rows, cols] = high
        out_ref[2 * rows :, cols] = low
        cols = slice(scale * wrap.shape[1], (scale + 1) * wrap.shape[1])
        th_ref[:, cols], tl_ref[:, cols] = split(spread(wrap, scale))


COS1, COS3 = math.cos(math.pi / 8), math.cos(3 * math.pi / 8)


def real_sixteen(h0, h8, x, y):
    a, b = h0 + h8, h0 - h8
    c, d = x[2] + x[6], (x[2] - x[6]) * ROOT_HALF
    even = [a + x[4] + c, b + d, a - x[4], b - d, a + x[4] - c]
    e, f = x[1] - x[7], x[3] - x[5]
    g, h = x[1] + x[7], x[3] + x[5]
    odd = [g + h, e * COS1 + f * COS3, (g - h) * ROOT_HALF, e * COS3 - f * COS1]
    cosines = [even[n] + odd[n] for n in range(4)] + [even[4]]
    cosines += [even[n] - odd[n] for n in (3, 2, 1, 0)]
    k = (y[2] + y[6]) * ROOT_HALF
    even = [None, k + y[4], y[2] - y[6], k - y[4]]
    e, f = y[1] + y[7], y[3] + y[5]
    odd = [
        None,
        e * COS3 + f * COS1,
        (y[1] - y[7] + y[3] - y[5]) * ROOT_HALF,
        e * COS1 - f * COS3,
        y[1] - y[7] - y[3] + y[5],
    ]
    sines = [None] + [even[n] + odd[n] for n in (1, 2, 3)] + [odd[4]]
    sines += [odd[n] - even[n] for n in (3, 2, 1)]
    out = [None] * 16
    out[0], out[8] = cosines[0], cosines[8]
    for n in range(1, 8):
        out[n] = cosines[n] - sines[n]
        out[16 - n] = cosines[n] + sines[n]
    return out


def column_kernel(
    rows_ref, across_ref, hat_ref, th_ref, tl_ref, tables_ref,
    out_ref, qt_ref, qh_ref, ql_ref, corr_ref, va_ref, vb_ref, o_ref, f_ref, sem, table_sem,
):
    tiles = tables_ref.shape[0] - 1
    fetches = [
        pltpu.make_async_copy(tables_ref.at[n], f_ref.at[n], table_sem.at[n])
        for n in range(tiles + 1)
    ]
    for fetch in fetches:
        fetch.start()
    bands = rows_ref.shape[0]
    width = qh_ref.shape[1]
    per_scale = width // NSCALE
    keys = LANES // 2
    half = CLASSES // 2

    for i in range(bands):
        high, low = split(rows_ref[i])
        product = dot(jnp.concatenate([high, low, high], axis=0), across_ref[...], 0, 0)
        for lane in range(width // LANES):
            cols = slice(lane * LANES, (lane + 1) * LANES)
            qt_ref[0, lane, i * LANES : (i + 1) * LANES, :] = product[:LANES, cols]
            qt_ref[1, lane, i * LANES : (i + 1) * LANES, :] = product[LANES:, cols]
    edge = jnp.zeros((width, LANES), F32)
    fetches[0].wait()
    for slot in range(half):
        halves = []
        for m in (slot, CLASSES - slot if slot else half):
            parts = []
            for lane in range(width // LANES):
                here = pl.ds(m, keys, stride=CLASSES)
                pair = [qt_ref[ri, lane, here, :] for ri in range(2)]
                parts.append(jnp.concatenate(pair, axis=0).T)
            halves.append(jnp.concatenate(parts, axis=0))
        high, low = split(jnp.concatenate(halves, axis=1))
        edge = edge + dot3(
            high, low, f_ref[0, 0, slot, :, :LANES], f_ref[0, 1, slot, :, :LANES]
        )
        for at, m in enumerate((slot, CLASSES - slot if slot else half)):
            q = halves[at]
            turned = pltpu.roll(q, keys, 1)
            lanes = slice(at * LANES, (at + 1) * LANES)
            for scale in range(NSCALE):
                mine = slice(scale * per_scale, (scale + 1) * per_scale)
                high, low = split(
                    q[mine] * hat_ref[scale, 0, m : m + 1, :]
                    + turned[mine] * hat_ref[scale, 1, m : m + 1, :]
                )
                qh_ref[slot, mine, lanes] = high
                ql_ref[slot, mine, lanes] = low
    high, low = split(edge)
    for scale in range(NSCALE):
        mine = slice(scale * per_scale, (scale + 1) * per_scale)
        cols = slice(scale * 2 * LANES, (scale + 1) * 2 * LANES)
        corr_ref[mine, :] = dot3(high[mine], low[mine], th_ref[:, cols], tl_ref[:, cols])

    def copy(tile, at):
        first = (at * tiles + tile) * LANES
        return pltpu.make_async_copy(
            o_ref.at[tile % 2, at], out_ref.at[:, first : first + LANES], sem.at[tile % 2, at]
        )

    step = 8

    def combine(v_ref, tile, first, last):
        for n in range(first, last, step):
            here = slice(n, n + step)
            x = [v_ref[m, here, :LANES] for m in range(half)]
            y = [v_ref[m, here, LANES:] for m in range(half)]
            outs = real_sixteen(x[0], y[0], x, y)
            if tile == 0:
                outs[0] = outs[0] - corr_ref[here, :LANES]
            if tile == tiles - 1:
                outs[-1] = outs[-1] - corr_ref[here, LANES:]
            for at in range(CLASSES):
                o_ref[tile % 2, at, here, :] = outs[at]

    share = width // half
    for tile in range(tiles + 1):
        now, before = (va_ref, vb_ref) if tile % 2 == 0 else (vb_ref, va_ref)
        if tile >= 3:
            for at in range(CLASSES):
                copy(tile - 3, at).wait()
        if tile < tiles:
            fetches[tile + 1].wait()
        for m in range(half):
            if tile < tiles:
                now[m] = dot3(
                    qh_ref[m], ql_ref[m], f_ref[tile + 1, 0, m], f_ref[tile + 1, 1, m]
                )
            if tile > 0:
                combine(before, tile - 1, m * share, (m + 1) * share)
        if tile > 0:
            for at in range(CLASSES):
                copy(tile - 1, at).start()
    for tile in range(max(tiles - 2, 0), tiles):
        for at in range(CLASSES):
            copy(tile, at).wait()


def kernel_device(
    vis, vis_pos, vis_w, subgrid_tile, subgrid_group, subgrid_col, grid_kernel, scale_kernels
):
    nr = lax.axis_size("row")
    nc = lax.axis_size("col")
    row, col = lax.axis_index("row"), lax.axis_index("col")
    tile_width = G // nc
    stride = G // nr
    cols_here = G // (nr * nc)
    window = cols_here + 2 * HALO
    per_class = window // RADIX
    part = G // RADIX
    subs = subgrid_col.shape[0]
    width = NSCALE * cols_here

    info = jnp.concatenate([subgrid_tile[:, 0], subgrid_group[:, 0], subgrid_col]).astype(F32)
    info = jnp.pad(info, (0, LANES - info.shape[0]))
    here = vis.shape[1]
    packed = jnp.concatenate(
        [
            jnp.concatenate(
                [jnp.stack(rotated_visibilities(vis, vis_w)), vis_pos.astype(F32)], axis=0
            ),
            jnp.broadcast_to(info[None], (4, LANES)),
        ],
        axis=1,
    )
    shifts = [[(i, (i + d) % nc) for i in range(nc)] for d in range(1, nc)]
    packs = [packed] + [lax.ppermute(packed, "col", s) for s in shifts]

    def grid_block(pack):
        return pl.pallas_call(
            subgrid_kernel,
            out_shape=jax.ShapeDtypeStruct((subs // 2 * SUB, LANES), F32),
            cost_estimate=pl.CostEstimate(
                flops=2 * 4 * subs * VPS * 4 * SUB * 2 * SUB,
                bytes_accessed=2**21,
                transcendentals=0,
            ),
            compiler_params=pltpu.CompilerParams(vmem_limit_bytes=32 * 2**20),
            name="subgrids",
        )(pack, grid_kernel)

    blocks = [grid_block(pack) for pack in packs[:2]]
    blocks[1], *packs[2:] = lax.optimization_barrier((blocks[1], *packs[2:]))
    blocks += [grid_block(pack) for pack in packs[2:]]
    infos = jnp.concatenate([pack[:1, here:] for pack in packs], axis=0)

    inner = np.arange(part)
    cosine, sine = turn(
        (stride * np.arange(nr)[:, None] + RADIX * np.arange(per_class)[None, :]).reshape(-1, 1)
        * inner,
        G,
    )
    tables = np.stack(split_table(np.concatenate([cosine, sine], axis=0)))
    first_q = np.arange(nc)[:, None, None] * cols_here - HALO
    cosine, sine = turn((first_q + np.arange(RADIX)) * inner[None, :, None], G)
    turns = np.concatenate([cosine, sine], axis=2).astype(np.float32)
    turns = lax.dynamic_index_in_dim(jnp.asarray(turns), col, 0, keepdims=False)
    vmem = pl.BlockSpec(memory_space=pltpu.VMEM)
    rows = pl.pallas_call(
        lambda *refs: row_kernel(
            *refs, blocks=nc, part=part, per_class=per_class, tile_width=tile_width
        ),
        out_shape=jax.ShapeDtypeStruct((nr, window, 2 * LANES), F32),
        in_specs=[pl.BlockSpec(memory_space=pltpu.SMEM)]
        + [vmem] * (nc + 1)
        + [pl.BlockSpec(memory_space=pl.ANY)],
        out_specs=vmem,
        scratch_shapes=[
            pltpu.VMEM((G, LANES), F32),
            pltpu.VMEM((G, LANES), F32),
            pltpu.VMEM((RADIX, part, 2 * LANES), BF16),
            pltpu.VMEM((RADIX, part, 2 * LANES), BF16),
            pltpu.VMEM(tables.shape, BF16),
            pltpu.SemaphoreType.DMA,
        ],
        compiler_params=pltpu.CompilerParams(vmem_limit_bytes=48 * 2**20),
        name="rows",
    )(infos, *blocks, turns, jnp.asarray(tables))

    rows = lax.all_to_all(rows, "row", split_axis=0, concat_axis=0, tiled=True)

    place = (RADIX * np.arange(per_class)[None, :] + np.arange(RADIX)[:, None]).reshape(-1)
    distance = place[:, None] - np.arange(cols_here)[None, :]
    distance = np.where((distance >= 0) & (distance < KW), distance, -1)
    at_q = (row * nc + col) * cols_here - HALO + jnp.asarray(place, jnp.int32)
    inside = ((at_q >= 0) & (at_q < G)).astype(F32) * (1.0 / G)
    wrap = np.full((LANES, 2 * LANES), -1)
    for e in range(HALO):
        for p in range(e + 1):
            wrap[e, p] = e - p
        for j in range(e, HALO):
            wrap[HALO + e, 2 * LANES - HALO + j] = e + 2 * HALO - j
    across, th, tl = pl.pallas_call(
        band_kernel,
        out_shape=[jax.ShapeDtypeStruct((3 * window, width), BF16)]
        + [jax.ShapeDtypeStruct((LANES, NSCALE * 2 * LANES), BF16)] * 2,
        in_specs=[pl.BlockSpec(memory_space=pltpu.SMEM)] + [vmem] * 3,
        out_specs=[vmem] * 3,
        compiler_params=pltpu.CompilerParams(vmem_limit_bytes=32 * 2**20),
        name="bands",
    )(
        scale_kernels,
        jnp.asarray(distance, jnp.int32),
        jnp.asarray(wrap, jnp.int32),
        inside[:, None],
    )
    per_band = LANES // CLASSES // nc
    keys = (
        np.arange(nr)[:, None, None] * stride
        + np.arange(nc)[None, :, None] * (stride // nc)
        + np.arange(per_band)[None, None, :] * CLASSES
    ).reshape(-1)
    k_of = np.arange(CLASSES)[:, None] + keys[None, :]
    cosine, sine = turn((np.arange(KW) - HALO)[:, None, None] * k_of, G)
    hat_table = np.stack(
        [
            np.concatenate([cosine, cosine], axis=2),
            np.concatenate([-sine, sine], axis=2),
        ],
        axis=1,
    )
    hat = jnp.dot(
        scale_kernels, jnp.asarray(hat_table.reshape(KW, -1), F32), precision=HIGHEST
    ).reshape(NSCALE, 2, CLASSES, 2 * keys.size)
    near = np.arange(-HALO, HALO)
    cosine, sine = turn(k_of[:, :, None] * near, G)
    edge = np.zeros((CLASSES, 2 * keys.size, 2 * LANES))
    edge[:, : keys.size, : 2 * HALO] = cosine
    edge[:, keys.size :, : 2 * HALO] = -sine
    half = CLASSES // 2
    others = [CLASSES - m if m else half for m in range(half)]
    edge = np.concatenate([edge[:half], edge[others]], axis=1)
    span = G // CLASSES
    tiles = span // LANES
    cosine, sine = turn(k_of[:, :, None] * np.arange(span), G)
    real = np.concatenate([cosine, -sine], axis=1)
    imag = np.concatenate([sine, cosine], axis=1)
    none = np.zeros_like(real[0])
    table = [np.block([[real[0], none], [none, real[half]]])]
    for m in range(1, half):
        other = CLASSES - m
        table.append(np.block([[real[m], imag[m]], [real[other], -imag[other]]]))
    table = np.stack(table).reshape(half, 4 * keys.size, 2, tiles, LANES)
    table = table.transpose(3, 0, 1, 2, 4).reshape(tiles, half, 4 * keys.size, 2 * LANES)
    tables = np.stack(split_table(np.concatenate([edge[None], table], axis=0)), axis=1)
    operands = (rows, across, hat, th, tl)
    out = pl.pallas_call(
        column_kernel,
        out_shape=jax.ShapeDtypeStruct((width, G), F32),
        in_specs=[vmem] * len(operands) + [pl.BlockSpec(memory_space=pl.ANY)],
        out_specs=pl.BlockSpec(memory_space=pl.ANY),
        scratch_shapes=[
            pltpu.VMEM((2, width // LANES, nr * LANES, LANES), F32),
            pltpu.VMEM((half, width, 4 * keys.size), BF16),
            pltpu.VMEM((half, width, 4 * keys.size), BF16),
            pltpu.VMEM((width, 2 * LANES), F32),
            pltpu.VMEM((half, width, 2 * LANES), F32),
            pltpu.VMEM((half, width, 2 * LANES), F32),
            pltpu.VMEM((2, CLASSES, width, LANES), F32),
            pltpu.VMEM(tables.shape, BF16),
            pltpu.SemaphoreType.DMA((2, CLASSES)),
            pltpu.SemaphoreType.DMA((tables.shape[0],)),
        ],
        compiler_params=pltpu.CompilerParams(vmem_limit_bytes=56 * 2**20),
        name="columns",
    )(*operands, jnp.asarray(tables))
    return out.reshape(NSCALE, cols_here, G)


def solution(mesh):
    nr, nc = mesh.shape["row"], mesh.shape["col"]
    fits = nr == RADIX and nc * SUB == LANES
    return jax.shard_map(
        kernel_device if fits else general_device,
        mesh=mesh,
        in_specs=(
            P(None, ("row", "col")),
            P(None, ("row", "col")),
            P(("row", "col")),
            P(("row", "col"), None),
            P(("row", "col"), None),
            P(("row", "col")),
            P(),
            P(),
        ),
        out_specs=P(None, ("row", "col"), None),
        check_vma=False,
    )
```

```python
import math

import jax
import jax.numpy as jnp
import numpy as np
from jax import lax
from jax.experimental import pallas as pl
from jax.experimental.pallas import tpu as pltpu
from jax.sharding import PartitionSpec as P

G = 8192
SUB = 32
SUP = 8
OVER = 8
VPS = 256
WSTEPS = 1024
KW = 33
NSCALE = 2
HALO = (KW - 1) // 2
RADIX = 8
CLASSES = 16
LANES = 128

HIGHEST = lax.Precision.HIGHEST
F32 = jnp.float32
BF16 = jnp.bfloat16
ROOT_HALF = math.sqrt(0.5)


def with_halo(array, sides, width):
    for axis, dim in sides:
        count, length = (lax.axis_size(axis), array.shape[dim])
        up = [(i, (i + 1) % count) for i in range(count - 1)]
        down = [(j, i) for i, j in up]
        last = lax.slice_in_dim(array, length - width, length, axis=dim)
        initial = lax.slice_in_dim(array, 0, width, axis=dim)
        before = lax.ppermute(last, axis, up)
        after = lax.ppermute(initial, axis, down)
        array = jnp.concatenate([before, array, after], axis=dim)
    return array


def kernel_taps(positions, grid_kernel):
    cell_index = positions // OVER
    fraction = positions % OVER
    onehot = (fraction[:, None] == jnp.arange(OVER, dtype=jnp.int32)[None, :]).astype(
        grid_kernel.dtype
    )
    values = jnp.dot(onehot, grid_kernel, precision=HIGHEST)
    offset = jnp.arange(SUB, dtype=jnp.int32)[None, :] - cell_index[:, None]
    result = jnp.zeros(offset.shape, grid_kernel.dtype)
    for tap_index in range(SUP):
        result = result + jnp.where(offset == tap_index, values[:, tap_index : tap_index + 1], 0.0)
    return result


def rotated_visibilities(vis_block, phase_steps):
    angles = phase_steps.astype(vis_block.dtype) * (2.0 * math.pi / WSTEPS)
    cosine = jnp.cos(angles)
    sine_part = jnp.sin(angles)
    return (
        vis_block[0] * cosine + vis_block[1] * sine_part,
        vis_block[1] * cosine - vis_block[0] * sine_part,
    )


def make_subgrids(vis_block, pos_block, phase_steps, grid_kernel, number):
    along_rows = kernel_taps(pos_block[0], grid_kernel).reshape(number, VPS, SUB)
    along_cols = kernel_taps(pos_block[1], grid_kernel).reshape(number, VPS, SUB)
    rotated_real, rotated_imag = rotated_visibilities(vis_block, phase_steps)
    weighted_real = along_rows * rotated_real.reshape(number, VPS, 1)
    weighted_imag = along_rows * rotated_imag.reshape(number, VPS, 1)
    sub_real = jnp.einsum("sja,sjb->sab", weighted_real, along_cols, precision=HIGHEST)
    sub_imag = jnp.einsum("sja,sjb->sab", weighted_imag, along_cols, precision=HIGHEST)
    return (sub_real, sub_imag)


def dft_table(length):
    positions = jnp.arange(length, dtype=jnp.int32)
    product = positions[:, None] * positions[None, :] % length
    angles = product.astype(jnp.float32) * (2.0 * math.pi / length)
    return (jnp.cos(angles), jnp.sin(angles))


def transform_last(real_part, imag_part, real_only):
    length = real_part.shape[-1]
    factor_one = 2 ** ((length.bit_length() - 1) // 2)
    factor_two = length // factor_one
    leading = real_part.shape[:-1]
    real_part = real_part.reshape(leading + (factor_one, factor_two))
    imag_part = imag_part.reshape(leading + (factor_one, factor_two))
    cos_one, sin_one = dft_table(factor_one)
    section_real = jnp.einsum(
        "...ab,ak->...kb", real_part, cos_one, precision=HIGHEST
    ) - jnp.einsum("...ab,ak->...kb", imag_part, sin_one, precision=HIGHEST)
    section_imag = jnp.einsum(
        "...ab,ak->...kb", real_part, sin_one, precision=HIGHEST
    ) + jnp.einsum("...ab,ak->...kb", imag_part, cos_one, precision=HIGHEST)
    outer_index = (
        jnp.arange(factor_one, dtype=jnp.int32)[:, None]
        * jnp.arange(factor_two, dtype=jnp.int32)[None, :]
        % length
    )
    twiddle = outer_index.astype(jnp.float32) * (2.0 * math.pi / length)
    twiddle_cos = jnp.cos(twiddle)
    twiddle_sin = jnp.sin(twiddle)
    turned_real = section_real * twiddle_cos - section_imag * twiddle_sin
    turned_imag = section_real * twiddle_sin + section_imag * twiddle_cos
    cos_two, sin_two = dft_table(factor_two)
    result_real = jnp.einsum(
        "...kb,bq->...qk", turned_real, cos_two, precision=HIGHEST
    ) - jnp.einsum("...kb,bq->...qk", turned_imag, sin_two, precision=HIGHEST)
    result_real = result_real.reshape(leading + (length,))
    if real_only:
        return result_real
    result_imag = jnp.einsum(
        "...kb,bq->...qk", turned_real, sin_two, precision=HIGHEST
    ) + jnp.einsum("...kb,bq->...qk", turned_imag, cos_two, precision=HIGHEST)
    return (result_real, result_imag.reshape(leading + (length,)))


def band_matrix(kernel_row, height, columns):
    distance = (
        jnp.arange(height, dtype=jnp.int32)[:, None] - jnp.arange(columns, dtype=jnp.int32)[None, :]
    )
    matrix = jnp.zeros((height, columns), jnp.float32)
    for tap_index in range(KW):
        matrix = matrix + jnp.where(distance == tap_index, kernel_row[tap_index], 0.0)
    return matrix


def smooth_along_rows(field, kernel_row):
    height = field.shape[0]
    length = field.shape[1]
    halo_width = (KW - 1) // 2
    block_size = min(128, length)
    blocks = length // block_size
    padded = jnp.pad(field, ((0, 0), (halo_width, block_size - halo_width)))
    framed = padded.reshape(height, blocks + 1, block_size)
    windows = jnp.concatenate([framed[:, :-1, :], framed[:, 1:, : 2 * halo_width]], axis=2)
    matrix = band_matrix(kernel_row, block_size + 2 * halo_width, block_size)
    return jnp.einsum("rni,io->rno", windows, matrix, precision=HIGHEST).reshape(height, length)


def smooth_across(field, kernel_row):
    height = field.shape[0]
    inner_rows = height - (KW - 1)
    matrix = band_matrix(kernel_row, height, inner_rows)
    return jnp.einsum("ry,rx->xy", field, matrix, precision=HIGHEST)


def slot_numbers(bucket_keys, buckets, capacity):
    count = bucket_keys.shape[0]
    index = jnp.arange(count, dtype=jnp.int32)
    same = (bucket_keys[:, None] == bucket_keys[None, :]) & (index[None, :] < index[:, None])
    return bucket_keys * capacity + jnp.sum(same.astype(jnp.int32), axis=1)


def place_blocks(piece_real, piece_imag, owner, start, buckets, width):
    count = piece_real.shape[0]
    piece_rows = piece_real.shape[1] // SUB
    step = math.gcd(count, 32)
    turns = count // step
    piece_real = piece_real.reshape(turns, step, piece_rows, SUB)
    piece_imag = piece_imag.reshape(turns, step, piece_rows, SUB)
    owner = owner.reshape(turns, step)
    start = start.reshape(turns, step)
    column_index = jnp.arange(width, dtype=jnp.int32)
    sub_index = jnp.arange(SUB, dtype=jnp.int32)
    bucket_index = jnp.arange(buckets, dtype=jnp.int32)

    def add_block(carry, block):
        block_real, block_imag, block_owner, block_start = block
        shift = (
            column_index[None, None, :] == block_start[:, None, None] + sub_index[None, :, None]
        ).astype(jnp.float32)
        pick = (block_owner[:, None] == bucket_index[None, :]).astype(jnp.float32)
        moved_real = jnp.einsum("sab,sbc->sac", block_real, shift, precision=HIGHEST)
        moved_imag = jnp.einsum("sab,sbc->sac", block_imag, shift, precision=HIGHEST)
        total_real = carry[0] + jnp.einsum("sg,sac->gac", pick, moved_real, precision=HIGHEST)
        total_imag = carry[1] + jnp.einsum("sg,sac->gac", pick, moved_imag, precision=HIGHEST)
        return ((total_real, total_imag), None)

    empty = jnp.zeros((buckets, piece_rows, width), jnp.float32)
    (placed_real, placed_imag), unused = lax.scan(
        add_block, (empty, empty), (piece_real, piece_imag, owner, start)
    )
    return (placed_real, placed_imag)


def general_device(
    vis, vis_pos, vis_w, subgrid_tile, subgrid_group, subgrid_col, grid_kernel, scale_kernels
):
    row_devices = lax.axis_size("row")
    col_devices = lax.axis_size("col")
    band_rows = G // row_devices
    tile_width = G // col_devices
    group_rows = band_rows // col_devices
    pencil_cols = G // (row_devices * col_devices)
    piece_rows = min(group_rows, SUB)
    pieces = SUB // piece_rows
    subgrids_here = subgrid_col.shape[0]
    batch_size = min(16, subgrids_here)
    batches = subgrids_here // batch_size
    batch_vis = batch_size * VPS

    def grid_batch(step_index):
        start = step_index * batch_vis
        vis_block = lax.dynamic_slice_in_dim(vis, start, batch_vis, 1)
        pos_block = lax.dynamic_slice_in_dim(vis_pos, start, batch_vis, 1)
        phase_block = lax.dynamic_slice_in_dim(vis_w, start, batch_vis, 0)
        sub_real, sub_imag = make_subgrids(
            vis_block, pos_block, phase_block, grid_kernel, batch_size
        )
        return (sub_real.reshape(batch_size, SUB * SUB), sub_imag.reshape(batch_size, SUB * SUB))

    sub_real, sub_imag = lax.map(grid_batch, jnp.arange(batches, dtype=jnp.int32))
    sub_real = sub_real.reshape(subgrids_here, SUB * SUB)
    sub_imag = sub_imag.reshape(subgrids_here, SUB * SUB)
    tile_index = subgrid_tile[:, 0]
    groups = subgrid_group[:, 0]
    groups_used = col_devices - pieces + 1
    most_group = min(subgrids_here, 3 * ((subgrids_here + groups_used - 1) // groups_used) // 2)
    capacity = pieces * most_group
    owners = (groups[:, None] + jnp.arange(pieces, dtype=jnp.int32)[None, :]).reshape(-1)
    starts = jnp.broadcast_to(
        (tile_index * tile_width + subgrid_col)[:, None], (subgrids_here, pieces)
    ).reshape(-1)
    slot_index = slot_numbers(owners, col_devices, capacity)
    piece_real = sub_real.reshape(subgrids_here * pieces, piece_rows * SUB)
    piece_imag = sub_imag.reshape(subgrids_here * pieces, piece_rows * SUB)
    send_real = (
        jnp.zeros((col_devices * capacity, piece_rows * SUB), jnp.float32)
        .at[slot_index]
        .set(piece_real)
    )
    send_imag = (
        jnp.zeros((col_devices * capacity, piece_rows * SUB), jnp.float32)
        .at[slot_index]
        .set(piece_imag)
    )
    send_start = jnp.zeros((col_devices * capacity,), jnp.int32).at[slot_index].set(starts)
    recv_real, recv_imag, recv_start = (
        lax.all_to_all(send_real, "col", split_axis=0, concat_axis=0, tiled=True),
        lax.all_to_all(send_imag, "col", split_axis=0, concat_axis=0, tiled=True),
        lax.all_to_all(send_start, "col", split_axis=0, concat_axis=0, tiled=True),
    )
    placed_real, placed_imag = place_blocks(
        recv_real,
        recv_imag,
        recv_start // tile_width,
        recv_start % tile_width,
        col_devices,
        tile_width,
    )
    widen = ((0, group_rows - piece_rows), (0, 0))
    slab_real = jnp.pad(placed_real.transpose(1, 0, 2).reshape(piece_rows, G), widen)
    slab_imag = jnp.pad(placed_imag.transpose(1, 0, 2).reshape(piece_rows, G), widen)
    rows_real, rows_imag = transform_last(slab_real, slab_imag, False)
    cols_real, cols_imag = (
        lax.all_to_all(
            lax.all_to_all(rows_real, "row", split_axis=1, concat_axis=0, tiled=True),
            "col",
            split_axis=1,
            concat_axis=0,
            tiled=True,
        ),
        lax.all_to_all(
            lax.all_to_all(rows_imag, "row", split_axis=1, concat_axis=0, tiled=True),
            "col",
            split_axis=1,
            concat_axis=0,
            tiled=True,
        ),
    )

    def reorder(field):
        return (
            field.reshape(col_devices, row_devices, group_rows, pencil_cols)
            .transpose(3, 1, 0, 2)
            .reshape(pencil_cols, G)
        )

    image = transform_last(reorder(cols_real), reorder(cols_imag), True) * (1.0 / G)
    halo_width = (KW - 1) // 2
    results = []
    padded = with_halo(image, ((("row", "col"), 0),), halo_width)
    for scale_index in range(NSCALE):
        vertical = smooth_along_rows(padded, scale_kernels[scale_index])
        results.append(smooth_across(vertical, scale_kernels[scale_index]))
    return jnp.stack(results)


def split(value):
    high = value.astype(BF16)
    return high, (value - high.astype(F32)).astype(BF16)


def split_table(table):
    table = np.asarray(table, np.float64)
    high = table.astype(BF16)
    return high, (table - high.astype(np.float64)).astype(BF16)


def turn(steps, length):
    angle = 2.0 * np.pi * (np.asarray(steps, np.int64) % length) / length
    return np.cos(angle), np.sin(angle)


def dot(left, right, left_dim=1, right_dim=0):
    return lax.dot_general(
        left, right, (((left_dim,), (right_dim,)), ((), ())), preferred_element_type=F32
    )


def dot3(left_high, left_low, right_high, right_low, left_dim=1, right_dim=0):
    return (
        dot(left_high, right_high, left_dim, right_dim)
        + dot(left_high, right_low, left_dim, right_dim)
        + dot(left_low, right_high, left_dim, right_dim)
    )


def subgrid_kernel(packed_ref, taps_ref, out_ref):
    span = 2 * VPS
    pairs = out_ref.shape[0] // SUB
    diagonal = lax.broadcasted_iota(jnp.int32, (OVER, SUP), 0) == lax.broadcasted_iota(
        jnp.int32, (OVER, SUP), 1
    )
    table = [
        jnp.sum(jnp.where(diagonal, taps_ref[s : s + 1, :], 0.0), axis=1, keepdims=True)
        for s in range(OVER)
    ]

    def taps(position):
        step = position & (OVER - 1)
        cell = position >> (OVER.bit_length() - 1)
        values = jnp.zeros((SUP, span), F32)
        for s in range(OVER):
            values = jnp.where(step == s, table[s], values)
        offset = lax.broadcasted_iota(jnp.int32, (SUB, span), 0) - cell
        result = jnp.zeros((SUB, span), F32)
        for t in range(SUP):
            result = jnp.where(offset == t, values[t : t + 1, :], result)
        return result

    first = lax.broadcasted_iota(jnp.int32, (SUB, LANES), 1) < LANES // 2

    def pair(p, carry):
        here = pl.ds(pl.multiple_of(p * span, span), span)
        along_rows = taps(packed_ref[2:3, here].astype(jnp.int32))
        along_cols = taps(packed_ref[3:4, here].astype(jnp.int32))
        weighted = jnp.concatenate(
            [along_rows * packed_ref[0:1, here], along_rows * packed_ref[1:2, here]], axis=0
        )
        weighted = jnp.concatenate(split(weighted), axis=0)
        cols = jnp.concatenate(split(along_cols), axis=0)
        sums = []
        for s in range(2):
            part = slice(s * VPS, (s + 1) * VPS)
            product = dot(cols[:, part], weighted[:, part], 1, 1)
            total = product[:SUB] + product[SUB:]
            sums.append(total + pltpu.roll(total, LANES // 2, 1))
        out_ref[pl.ds(pl.multiple_of(p * SUB, SUB), SUB), :] = jnp.where(first, sums[0], sums[1])
        return carry

    lax.fori_loop(0, pairs, pair, 0, unroll=8)


def radix_eight(real, imag):
    def four(r, i):
        a, b = (r[0] + r[2], i[0] + i[2])
        c, d = (r[0] - r[2], i[0] - i[2])
        e, f = (r[1] + r[3], i[1] + i[3])
        g, h = (r[1] - r[3], i[1] - i[3])
        return [(a + e, b + f), (c - h, d + g), (a - e, b - f), (c + h, d - g)]

    low = four(
        [real[n] + real[n + 4] for n in range(4)], [imag[n] + imag[n + 4] for n in range(4)]
    )
    dr = [real[n] - real[n + 4] for n in range(4)]
    di = [imag[n] - imag[n + 4] for n in range(4)]
    high = four(
        [dr[0], (dr[1] - di[1]) * ROOT_HALF, -di[2], (dr[3] + di[3]) * -ROOT_HALF],
        [di[0], (dr[1] + di[1]) * ROOT_HALF, dr[2], (dr[3] - di[3]) * ROOT_HALF],
    )
    return [(low, high)[c % 2][c // 2] for c in range(8)]


def row_kernel(info_ref, *refs, blocks, part, per_class, tile_width):
    xs = refs[:blocks]
    turn_ref, tables_ref = refs[blocks : blocks + 2]
    outs = refs[blocks + 2 : -6]
    real_ref, imag_ref, uh_ref, ul_ref, both_ref, sem = refs[-6:]
    fetch = pltpu.make_async_copy(tables_ref, both_ref, sem)
    fetch.start()
    rows = real_ref.shape[0]
    chunk = 256

    def clear(n, carry):
        here = pl.ds(pl.multiple_of(n * chunk, chunk), chunk)
        real_ref[here, :] = jnp.zeros((chunk, LANES), F32)
        imag_ref[here, :] = jnp.zeros((chunk, LANES), F32)
        return carry

    lax.fori_loop(0, rows // chunk, clear, 0)
    owner = lax.broadcasted_iota(jnp.int32, (SUB, LANES), 1) // SUB
    for b in range(blocks):
        pairs = xs[b].shape[0] // SUB

        def place(p, carry, b=b, pairs=pairs):
            piece = xs[b][pl.ds(pl.multiple_of(p * SUB, SUB), SUB), :]
            for s in range(2):
                number = 2 * p + s
                tile, group, start = (
                    info_ref[b, n * 2 * pairs + number].astype(jnp.int32) for n in range(3)
                )
                start = tile * tile_width + start
                for dest, at in ((real_ref, 2 * s), (imag_ref, 2 * s + 1)):
                    shift = (group * SUB + (LANES - at * SUB)) & (LANES - 1)
                    moved = jnp.where(owner == group, pltpu.roll(piece, shift, 1), 0.0)
                    dest[pl.ds(start, SUB), :] += moved
            return carry

        lax.fori_loop(0, pairs, place, 0, unroll=4)

    step = 16

    def classes(n, carry):
        first = pl.multiple_of(n * step, step)
        real = [real_ref[pl.ds(k * part + first, step), :] for k in range(RADIX)]
        imag = [imag_ref[pl.ds(k * part + first, step), :] for k in range(RADIX)]
        turns = turn_ref[pl.ds(first, step), :]
        for c, (ur, ui) in enumerate(radix_eight(real, imag)):
            cosine = turns[:, c : c + 1]
            sine = turns[:, RADIX + c : RADIX + c + 1]
            vr = ur * cosine - ui * sine
            vi = ur * sine + ui * cosine
            high, low = split(jnp.concatenate([vr, vi], axis=1))
            uh_ref[c, pl.ds(first, step), :] = high
            ul_ref[c, pl.ds(first, step), :] = low
        return carry

    lax.fori_loop(0, part // step, classes, 0, unroll=4)
    half = len(outs) * per_class
    fetch.wait()
    for c in range(RADIX):
        total = dot3(both_ref[0], both_ref[1], uh_ref[c], ul_ref[c])
        real = total[:half, :LANES] - total[half:, LANES:]
        imag = total[:half, LANES:] + total[half:, :LANES]
        here = slice(c * per_class, (c + 1) * per_class)
        for d, out_ref in enumerate(outs):
            mine = slice(d * per_class, (d + 1) * per_class)
            out_ref[here, :LANES] = real[mine]
            out_ref[here, LANES:] = imag[mine]


def band_kernel(taps_ref, across_ref, wrap_ref, inside_ref, out_ref, th_ref, tl_ref):
    def spread(index, scale):
        out = jnp.zeros(index.shape, F32)
        for u in range(KW):
            out = jnp.where(index == u, taps_ref[scale, u], out)
        return out

    across, wrap = across_ref[...], wrap_ref[...]
    rows = across.shape[0]
    for scale in range(NSCALE):
        cols = slice(scale * across.shape[1], (scale + 1) * across.shape[1])
        high, low = split(spread(across, scale) * inside_ref[...])
        out_ref[:rows, cols] = high
        out_ref[rows : 2 * rows, cols] = high
        out_ref[2 * rows :, cols] = low
        cols = slice(scale * wrap.shape[1], (scale + 1) * wrap.shape[1])
        th_ref[:, cols], tl_ref[:, cols] = split(spread(wrap, scale))


COS1, COS3 = math.cos(math.pi / 8), math.cos(3 * math.pi / 8)


def real_sixteen(h0, h8, x, y):
    a, b = h0 + h8, h0 - h8
    c, d = x[2] + x[6], (x[2] - x[6]) * ROOT_HALF
    even = [a + x[4] + c, b + d, a - x[4], b - d, a + x[4] - c]
    e, f = x[1] - x[7], x[3] - x[5]
    g, h = x[1] + x[7], x[3] + x[5]
    odd = [g + h, e * COS1 + f * COS3, (g - h) * ROOT_HALF, e * COS3 - f * COS1]
    cosines = [even[n] + odd[n] for n in range(4)] + [even[4]]
    cosines += [even[n] - odd[n] for n in (3, 2, 1, 0)]
    k = (y[2] + y[6]) * ROOT_HALF
    even = [None, k + y[4], y[2] - y[6], k - y[4]]
    e, f = y[1] + y[7], y[3] + y[5]
    odd = [
        None,
        e * COS3 + f * COS1,
        (y[1] - y[7] + y[3] - y[5]) * ROOT_HALF,
        e * COS1 - f * COS3,
        y[1] - y[7] - y[3] + y[5],
    ]
    sines = [None] + [even[n] + odd[n] for n in (1, 2, 3)] + [odd[4]]
    sines += [odd[n] - even[n] for n in (3, 2, 1)]
    out = [None] * 16
    out[0], out[8] = cosines[0], cosines[8]
    for n in range(1, 8):
        out[n] = cosines[n] - sines[n]
        out[16 - n] = cosines[n] + sines[n]
    return out


def column_kernel(
    row_ref, *refs,
):
    *parts, across_ref, hat_ref, th_ref, tl_ref, tables_ref = refs[:-11]
    out_ref, qt_ref, qh_ref, ql_ref, corr_ref, va_ref, vb_ref, o_ref, f_ref, sem, table_sem = refs[
        -11:
    ]
    tiles = tables_ref.shape[0] - 1
    fetches = [
        pltpu.make_async_copy(tables_ref.at[n], f_ref.at[n], table_sem.at[n])
        for n in range(tiles + 1)
    ]
    for fetch in fetches:
        fetch.start()
    bands = len(parts)
    width = qh_ref.shape[1]
    per_scale = width // NSCALE
    keys = LANES // 2
    half = CLASSES // 2

    for d, part in enumerate(parts):
        band = lax.rem(row_ref[0, 0] + (bands - d), bands)
        here = pl.ds(pl.multiple_of(band * LANES, LANES), LANES)
        high, low = split(part[...])
        product = dot(jnp.concatenate([high, low, high], axis=0), across_ref[...], 0, 0)
        for lane in range(width // LANES):
            cols = slice(lane * LANES, (lane + 1) * LANES)
            qt_ref[0, lane, here, :] = product[:LANES, cols]
            qt_ref[1, lane, here, :] = product[LANES:, cols]
    edge = jnp.zeros((width, LANES), F32)
    fetches[0].wait()
    for slot in range(half):
        halves = []
        for m in (slot, CLASSES - slot if slot else half):
            parts = []
            for lane in range(width // LANES):
                here = pl.ds(m, keys, stride=CLASSES)
                pair = [qt_ref[ri, lane, here, :] for ri in range(2)]
                parts.append(jnp.concatenate(pair, axis=0).T)
            halves.append(jnp.concatenate(parts, axis=0))
        high, low = split(jnp.concatenate(halves, axis=1))
        edge = edge + dot3(
            high, low, f_ref[0, 0, slot, :, :LANES], f_ref[0, 1, slot, :, :LANES]
        )
        for at, m in enumerate((slot, CLASSES - slot if slot else half)):
            q = halves[at]
            turned = pltpu.roll(q, keys, 1)
            lanes = slice(at * LANES, (at + 1) * LANES)
            for scale in range(NSCALE):
                mine = slice(scale * per_scale, (scale + 1) * per_scale)
                high, low = split(
                    q[mine] * hat_ref[scale, 0, m : m + 1, :]
                    + turned[mine] * hat_ref[scale, 1, m : m + 1, :]
                )
                qh_ref[slot, mine, lanes] = high
                ql_ref[slot, mine, lanes] = low
    high, low = split(edge)
    for scale in range(NSCALE):
        mine = slice(scale * per_scale, (scale + 1) * per_scale)
        cols = slice(scale * 2 * LANES, (scale + 1) * 2 * LANES)
        corr_ref[mine, :] = dot3(high[mine], low[mine], th_ref[:, cols], tl_ref[:, cols])

    def copy(tile, at):
        first = (at * tiles + tile) * LANES
        return pltpu.make_async_copy(
            o_ref.at[tile % 2, at], out_ref.at[:, first : first + LANES], sem.at[tile % 2, at]
        )

    step = 8

    def combine(v_ref, tile, first, last):
        for n in range(first, last, step):
            here = slice(n, n + step)
            x = [v_ref[m, here, :LANES] for m in range(half)]
            y = [v_ref[m, here, LANES:] for m in range(half)]
            outs = real_sixteen(x[0], y[0], x, y)
            if tile == 0:
                outs[0] = outs[0] - corr_ref[here, :LANES]
            if tile == tiles - 1:
                outs[-1] = outs[-1] - corr_ref[here, LANES:]
            for at in range(CLASSES):
                o_ref[tile % 2, at, here, :] = outs[at]

    share = width // half
    for tile in range(tiles + 1):
        now, before = (va_ref, vb_ref) if tile % 2 == 0 else (vb_ref, va_ref)
        if tile >= 3:
            for at in range(CLASSES):
                copy(tile - 3, at).wait()
        if tile < tiles:
            fetches[tile + 1].wait()
        for m in range(half):
            if tile < tiles:
                now[m] = dot3(
                    qh_ref[m], ql_ref[m], f_ref[tile + 1, 0, m], f_ref[tile + 1, 1, m]
                )
            if tile > 0:
                combine(before, tile - 1, m * share, (m + 1) * share)
        if tile > 0:
            for at in range(CLASSES):
                copy(tile - 1, at).start()
    for tile in range(max(tiles - 2, 0), tiles):
        for at in range(CLASSES):
            copy(tile, at).wait()


def kernel_device(
    vis, vis_pos, vis_w, subgrid_tile, subgrid_group, subgrid_col, grid_kernel, scale_kernels
):
    nr = lax.axis_size("row")
    nc = lax.axis_size("col")
    row, col = lax.axis_index("row"), lax.axis_index("col")
    tile_width = G // nc
    stride = G // nr
    cols_here = G // (nr * nc)
    window = cols_here + 2 * HALO
    per_class = window // RADIX
    part = G // RADIX
    subs = subgrid_col.shape[0]
    width = NSCALE * cols_here

    info = jnp.concatenate([subgrid_tile[:, 0], subgrid_group[:, 0], subgrid_col]).astype(F32)
    info = jnp.pad(info, (0, LANES - info.shape[0]))
    here = vis.shape[1]
    packed = jnp.concatenate(
        [
            jnp.concatenate(
                [jnp.stack(rotated_visibilities(vis, vis_w)), vis_pos.astype(F32)], axis=0
            ),
            jnp.broadcast_to(info[None], (4, LANES)),
        ],
        axis=1,
    )
    shifts = [[(i, (i + d) % nc) for i in range(nc)] for d in range(1, nc)]
    packs = [packed] + [lax.ppermute(packed, "col", s) for s in shifts]

    def grid_block(pack):
        return pl.pallas_call(
            subgrid_kernel,
            out_shape=jax.ShapeDtypeStruct((subs // 2 * SUB, LANES), F32),
            cost_estimate=pl.CostEstimate(
                flops=2 * 4 * subs * VPS * 4 * SUB * 2 * SUB,
                bytes_accessed=2**21,
                transcendentals=0,
            ),
            compiler_params=pltpu.CompilerParams(vmem_limit_bytes=32 * 2**20),
            name="subgrids",
        )(pack, grid_kernel)

    blocks = [grid_block(pack) for pack in packs[:2]]
    blocks[1], *packs[2:] = lax.optimization_barrier((blocks[1], *packs[2:]))
    blocks += [grid_block(pack) for pack in packs[2:]]
    infos = jnp.concatenate([pack[:1, here:] for pack in packs], axis=0)

    inner = np.arange(part)
    cosine, sine = turn(
        (stride * np.arange(nr)[:, None] + RADIX * np.arange(per_class)[None, :]).reshape(-1, 1)
        * inner,
        G,
    )
    tables = np.stack(split_table(np.concatenate([cosine, sine], axis=0)))
    first_q = (np.arange(nr)[:, None] * stride + np.arange(nc) * cols_here).reshape(-1, 1, 1) - HALO
    cosine, sine = turn((first_q + np.arange(RADIX)) * inner[None, :, None], G)
    turns = np.concatenate([cosine, sine], axis=2).astype(np.float32)
    turns = lax.dynamic_index_in_dim(jnp.asarray(turns), row * nc + col, 0, keepdims=False)
    vmem = pl.BlockSpec(memory_space=pltpu.VMEM)
    rows = pl.pallas_call(
        lambda *refs: row_kernel(
            *refs, blocks=nc, part=part, per_class=per_class, tile_width=tile_width
        ),
        out_shape=[jax.ShapeDtypeStruct((window, 2 * LANES), F32)] * nr,
        in_specs=[pl.BlockSpec(memory_space=pltpu.SMEM)]
        + [vmem] * (nc + 1)
        + [pl.BlockSpec(memory_space=pl.ANY)],
        out_specs=[vmem] * nr,
        scratch_shapes=[
            pltpu.VMEM((G, LANES), F32),
            pltpu.VMEM((G, LANES), F32),
            pltpu.VMEM((RADIX, part, 2 * LANES), BF16),
            pltpu.VMEM((RADIX, part, 2 * LANES), BF16),
            pltpu.VMEM(tables.shape, BF16),
            pltpu.SemaphoreType.DMA,
        ],
        compiler_params=pltpu.CompilerParams(vmem_limit_bytes=48 * 2**20),
        name="rows",
    )(infos, *blocks, turns, jnp.asarray(tables))

    rows = [rows[0]] + [
        lax.ppermute(rows[d], "row", [(i, (i + d) % nr) for i in range(nr)]) for d in range(1, nr)
    ]

    place = (RADIX * np.arange(per_class)[None, :] + np.arange(RADIX)[:, None]).reshape(-1)
    distance = place[:, None] - np.arange(cols_here)[None, :]
    distance = np.where((distance >= 0) & (distance < KW), distance, -1)
    at_q = (row * nc + col) * cols_here - HALO + jnp.asarray(place, jnp.int32)
    inside = ((at_q >= 0) & (at_q < G)).astype(F32) * (1.0 / G)
    wrap = np.full((LANES, 2 * LANES), -1)
    for e in range(HALO):
        for p in range(e + 1):
            wrap[e, p] = e - p
        for j in range(e, HALO):
            wrap[HALO + e, 2 * LANES - HALO + j] = e + 2 * HALO - j
    across, th, tl = pl.pallas_call(
        band_kernel,
        out_shape=[jax.ShapeDtypeStruct((3 * window, width), BF16)]
        + [jax.ShapeDtypeStruct((LANES, NSCALE * 2 * LANES), BF16)] * 2,
        in_specs=[pl.BlockSpec(memory_space=pltpu.SMEM)] + [vmem] * 3,
        out_specs=[vmem] * 3,
        compiler_params=pltpu.CompilerParams(vmem_limit_bytes=32 * 2**20),
        name="bands",
    )(
        scale_kernels,
        jnp.asarray(distance, jnp.int32),
        jnp.asarray(wrap, jnp.int32),
        inside[:, None],
    )
    per_band = LANES // CLASSES // nc
    keys = (
        np.arange(nr)[:, None, None] * stride
        + np.arange(nc)[None, :, None] * (stride // nc)
        + np.arange(per_band)[None, None, :] * CLASSES
    ).reshape(-1)
    k_of = np.arange(CLASSES)[:, None] + keys[None, :]
    cosine, sine = turn((np.arange(KW) - HALO)[:, None, None] * k_of, G)
    hat_table = np.stack(
        [
            np.concatenate([cosine, cosine], axis=2),
            np.concatenate([-sine, sine], axis=2),
        ],
        axis=1,
    )
    hat = jnp.dot(
        scale_kernels, jnp.asarray(hat_table.reshape(KW, -1), F32), precision=HIGHEST
    ).reshape(NSCALE, 2, CLASSES, 2 * keys.size)
    near = np.arange(-HALO, HALO)
    cosine, sine = turn(k_of[:, :, None] * near, G)
    edge = np.zeros((CLASSES, 2 * keys.size, 2 * LANES))
    edge[:, : keys.size, : 2 * HALO] = cosine
    edge[:, keys.size :, : 2 * HALO] = -sine
    half = CLASSES // 2
    others = [CLASSES - m if m else half for m in range(half)]
    edge = np.concatenate([edge[:half], edge[others]], axis=1)
    span = G // CLASSES
    tiles = span // LANES
    cosine, sine = turn(k_of[:, :, None] * np.arange(span), G)
    real = np.concatenate([cosine, -sine], axis=1)
    imag = np.concatenate([sine, cosine], axis=1)
    none = np.zeros_like(real[0])
    table = [np.block([[real[0], none], [none, real[half]]])]
    for m in range(1, half):
        other = CLASSES - m
        table.append(np.block([[real[m], imag[m]], [real[other], -imag[other]]]))
    table = np.stack(table).reshape(half, 4 * keys.size, 2, tiles, LANES)
    table = table.transpose(3, 0, 1, 2, 4).reshape(tiles, half, 4 * keys.size, 2 * LANES)
    tables = np.stack(split_table(np.concatenate([edge[None], table], axis=0)), axis=1)
    operands = (*rows, across, hat, th, tl)
    out = pl.pallas_call(
        column_kernel,
        out_shape=jax.ShapeDtypeStruct((width, G), F32),
        in_specs=[pl.BlockSpec(memory_space=pltpu.SMEM)]
        + [vmem] * len(operands)
        + [pl.BlockSpec(memory_space=pl.ANY)],
        out_specs=pl.BlockSpec(memory_space=pl.ANY),
        scratch_shapes=[
            pltpu.VMEM((2, width // LANES, nr * LANES, LANES), F32),
            pltpu.VMEM((half, width, 4 * keys.size), BF16),
            pltpu.VMEM((half, width, 4 * keys.size), BF16),
            pltpu.VMEM((width, 2 * LANES), F32),
            pltpu.VMEM((half, width, 2 * LANES), F32),
            pltpu.VMEM((half, width, 2 * LANES), F32),
            pltpu.VMEM((2, CLASSES, width, LANES), F32),
            pltpu.VMEM(tables.shape, BF16),
            pltpu.SemaphoreType.DMA((2, CLASSES)),
            pltpu.SemaphoreType.DMA((tables.shape[0],)),
        ],
        compiler_params=pltpu.CompilerParams(vmem_limit_bytes=56 * 2**20),
        name="columns",
    )(row.astype(jnp.int32).reshape(1, 1), *operands, jnp.asarray(tables))
    return out.reshape(NSCALE, cols_here, G)


def solution(mesh):
    nr, nc = mesh.shape["row"], mesh.shape["col"]
    fits = nr == RADIX and nc * SUB == LANES
    return jax.shard_map(
        kernel_device if fits else general_device,
        mesh=mesh,
        in_specs=(
            P(None, ("row", "col")),
            P(None, ("row", "col")),
            P(("row", "col")),
            P(("row", "col"), None),
            P(("row", "col"), None),
            P(("row", "col")),
            P(),
            P(),
        ),
        out_specs=P(None, ("row", "col"), None),
        check_vma=False,
    )
```

```python
import math

import jax
import jax.numpy as jnp
import numpy as np
from jax import lax
from jax.experimental import pallas as pl
from jax.experimental.pallas import tpu as pltpu
from jax.sharding import PartitionSpec as P

G = 8192
SUB = 32
SUP = 8
OVER = 8
VPS = 256
WSTEPS = 1024
KW = 33
NSCALE = 2
HALO = (KW - 1) // 2
RADIX = 8
CLASSES = 16
LANES = 128

HIGHEST = lax.Precision.HIGHEST
F32 = jnp.float32
BF16 = jnp.bfloat16
ROOT_HALF = math.sqrt(0.5)


def with_halo(array, sides, width):
    for axis, dim in sides:
        count, length = (lax.axis_size(axis), array.shape[dim])
        up = [(i, (i + 1) % count) for i in range(count - 1)]
        down = [(j, i) for i, j in up]
        last = lax.slice_in_dim(array, length - width, length, axis=dim)
        initial = lax.slice_in_dim(array, 0, width, axis=dim)
        before = lax.ppermute(last, axis, up)
        after = lax.ppermute(initial, axis, down)
        array = jnp.concatenate([before, array, after], axis=dim)
    return array


def kernel_taps(positions, grid_kernel):
    cell_index = positions // OVER
    fraction = positions % OVER
    onehot = (fraction[:, None] == jnp.arange(OVER, dtype=jnp.int32)[None, :]).astype(
        grid_kernel.dtype
    )
    values = jnp.dot(onehot, grid_kernel, precision=HIGHEST)
    offset = jnp.arange(SUB, dtype=jnp.int32)[None, :] - cell_index[:, None]
    result = jnp.zeros(offset.shape, grid_kernel.dtype)
    for tap_index in range(SUP):
        result = result + jnp.where(offset == tap_index, values[:, tap_index : tap_index + 1], 0.0)
    return result


def rotated_visibilities(vis_block, phase_steps):
    angles = phase_steps.astype(vis_block.dtype) * (2.0 * math.pi / WSTEPS)
    cosine = jnp.cos(angles)
    sine_part = jnp.sin(angles)
    return (
        vis_block[0] * cosine + vis_block[1] * sine_part,
        vis_block[1] * cosine - vis_block[0] * sine_part,
    )


def make_subgrids(vis_block, pos_block, phase_steps, grid_kernel, number):
    along_rows = kernel_taps(pos_block[0], grid_kernel).reshape(number, VPS, SUB)
    along_cols = kernel_taps(pos_block[1], grid_kernel).reshape(number, VPS, SUB)
    rotated_real, rotated_imag = rotated_visibilities(vis_block, phase_steps)
    weighted_real = along_rows * rotated_real.reshape(number, VPS, 1)
    weighted_imag = along_rows * rotated_imag.reshape(number, VPS, 1)
    sub_real = jnp.einsum("sja,sjb->sab", weighted_real, along_cols, precision=HIGHEST)
    sub_imag = jnp.einsum("sja,sjb->sab", weighted_imag, along_cols, precision=HIGHEST)
    return (sub_real, sub_imag)


def dft_table(length):
    positions = jnp.arange(length, dtype=jnp.int32)
    product = positions[:, None] * positions[None, :] % length
    angles = product.astype(jnp.float32) * (2.0 * math.pi / length)
    return (jnp.cos(angles), jnp.sin(angles))


def transform_last(real_part, imag_part, real_only):
    length = real_part.shape[-1]
    factor_one = 2 ** ((length.bit_length() - 1) // 2)
    factor_two = length // factor_one
    leading = real_part.shape[:-1]
    real_part = real_part.reshape(leading + (factor_one, factor_two))
    imag_part = imag_part.reshape(leading + (factor_one, factor_two))
    cos_one, sin_one = dft_table(factor_one)
    section_real = jnp.einsum(
        "...ab,ak->...kb", real_part, cos_one, precision=HIGHEST
    ) - jnp.einsum("...ab,ak->...kb", imag_part, sin_one, precision=HIGHEST)
    section_imag = jnp.einsum(
        "...ab,ak->...kb", real_part, sin_one, precision=HIGHEST
    ) + jnp.einsum("...ab,ak->...kb", imag_part, cos_one, precision=HIGHEST)
    outer_index = (
        jnp.arange(factor_one, dtype=jnp.int32)[:, None]
        * jnp.arange(factor_two, dtype=jnp.int32)[None, :]
        % length
    )
    twiddle = outer_index.astype(jnp.float32) * (2.0 * math.pi / length)
    twiddle_cos = jnp.cos(twiddle)
    twiddle_sin = jnp.sin(twiddle)
    turned_real = section_real * twiddle_cos - section_imag * twiddle_sin
    turned_imag = section_real * twiddle_sin + section_imag * twiddle_cos
    cos_two, sin_two = dft_table(factor_two)
    result_real = jnp.einsum(
        "...kb,bq->...qk", turned_real, cos_two, precision=HIGHEST
    ) - jnp.einsum("...kb,bq->...qk", turned_imag, sin_two, precision=HIGHEST)
    result_real = result_real.reshape(leading + (length,))
    if real_only:
        return result_real
    result_imag = jnp.einsum(
        "...kb,bq->...qk", turned_real, sin_two, precision=HIGHEST
    ) + jnp.einsum("...kb,bq->...qk", turned_imag, cos_two, precision=HIGHEST)
    return (result_real, result_imag.reshape(leading + (length,)))


def band_matrix(kernel_row, height, columns):
    distance = (
        jnp.arange(height, dtype=jnp.int32)[:, None] - jnp.arange(columns, dtype=jnp.int32)[None, :]
    )
    matrix = jnp.zeros((height, columns), jnp.float32)
    for tap_index in range(KW):
        matrix = matrix + jnp.where(distance == tap_index, kernel_row[tap_index], 0.0)
    return matrix


def smooth_along_rows(field, kernel_row):
    height = field.shape[0]
    length = field.shape[1]
    halo_width = (KW - 1) // 2
    block_size = min(128, length)
    blocks = length // block_size
    padded = jnp.pad(field, ((0, 0), (halo_width, block_size - halo_width)))
    framed = padded.reshape(height, blocks + 1, block_size)
    windows = jnp.concatenate([framed[:, :-1, :], framed[:, 1:, : 2 * halo_width]], axis=2)
    matrix = band_matrix(kernel_row, block_size + 2 * halo_width, block_size)
    return jnp.einsum("rni,io->rno", windows, matrix, precision=HIGHEST).reshape(height, length)


def smooth_across(field, kernel_row):
    height = field.shape[0]
    inner_rows = height - (KW - 1)
    matrix = band_matrix(kernel_row, height, inner_rows)
    return jnp.einsum("ry,rx->xy", field, matrix, precision=HIGHEST)


def slot_numbers(bucket_keys, buckets, capacity):
    count = bucket_keys.shape[0]
    index = jnp.arange(count, dtype=jnp.int32)
    same = (bucket_keys[:, None] == bucket_keys[None, :]) & (index[None, :] < index[:, None])
    return bucket_keys * capacity + jnp.sum(same.astype(jnp.int32), axis=1)


def place_blocks(piece_real, piece_imag, owner, start, buckets, width):
    count = piece_real.shape[0]
    piece_rows = piece_real.shape[1] // SUB
    step = math.gcd(count, 32)
    turns = count // step
    piece_real = piece_real.reshape(turns, step, piece_rows, SUB)
    piece_imag = piece_imag.reshape(turns, step, piece_rows, SUB)
    owner = owner.reshape(turns, step)
    start = start.reshape(turns, step)
    column_index = jnp.arange(width, dtype=jnp.int32)
    sub_index = jnp.arange(SUB, dtype=jnp.int32)
    bucket_index = jnp.arange(buckets, dtype=jnp.int32)

    def add_block(carry, block):
        block_real, block_imag, block_owner, block_start = block
        shift = (
            column_index[None, None, :] == block_start[:, None, None] + sub_index[None, :, None]
        ).astype(jnp.float32)
        pick = (block_owner[:, None] == bucket_index[None, :]).astype(jnp.float32)
        moved_real = jnp.einsum("sab,sbc->sac", block_real, shift, precision=HIGHEST)
        moved_imag = jnp.einsum("sab,sbc->sac", block_imag, shift, precision=HIGHEST)
        total_real = carry[0] + jnp.einsum("sg,sac->gac", pick, moved_real, precision=HIGHEST)
        total_imag = carry[1] + jnp.einsum("sg,sac->gac", pick, moved_imag, precision=HIGHEST)
        return ((total_real, total_imag), None)

    empty = jnp.zeros((buckets, piece_rows, width), jnp.float32)
    (placed_real, placed_imag), unused = lax.scan(
        add_block, (empty, empty), (piece_real, piece_imag, owner, start)
    )
    return (placed_real, placed_imag)


def general_device(
    vis, vis_pos, vis_w, subgrid_tile, subgrid_group, subgrid_col, grid_kernel, scale_kernels
):
    row_devices = lax.axis_size("row")
    col_devices = lax.axis_size("col")
    band_rows = G // row_devices
    tile_width = G // col_devices
    group_rows = band_rows // col_devices
    pencil_cols = G // (row_devices * col_devices)
    piece_rows = min(group_rows, SUB)
    pieces = SUB // piece_rows
    subgrids_here = subgrid_col.shape[0]
    batch_size = min(16, subgrids_here)
    batches = subgrids_here // batch_size
    batch_vis = batch_size * VPS

    def grid_batch(step_index):
        start = step_index * batch_vis
        vis_block = lax.dynamic_slice_in_dim(vis, start, batch_vis, 1)
        pos_block = lax.dynamic_slice_in_dim(vis_pos, start, batch_vis, 1)
        phase_block = lax.dynamic_slice_in_dim(vis_w, start, batch_vis, 0)
        sub_real, sub_imag = make_subgrids(
            vis_block, pos_block, phase_block, grid_kernel, batch_size
        )
        return (sub_real.reshape(batch_size, SUB * SUB), sub_imag.reshape(batch_size, SUB * SUB))

    sub_real, sub_imag = lax.map(grid_batch, jnp.arange(batches, dtype=jnp.int32))
    sub_real = sub_real.reshape(subgrids_here, SUB * SUB)
    sub_imag = sub_imag.reshape(subgrids_here, SUB * SUB)
    tile_index = subgrid_tile[:, 0]
    groups = subgrid_group[:, 0]
    groups_used = col_devices - pieces + 1
    most_group = min(subgrids_here, 3 * ((subgrids_here + groups_used - 1) // groups_used) // 2)
    capacity = pieces * most_group
    owners = (groups[:, None] + jnp.arange(pieces, dtype=jnp.int32)[None, :]).reshape(-1)
    starts = jnp.broadcast_to(
        (tile_index * tile_width + subgrid_col)[:, None], (subgrids_here, pieces)
    ).reshape(-1)
    slot_index = slot_numbers(owners, col_devices, capacity)
    piece_real = sub_real.reshape(subgrids_here * pieces, piece_rows * SUB)
    piece_imag = sub_imag.reshape(subgrids_here * pieces, piece_rows * SUB)
    send_real = (
        jnp.zeros((col_devices * capacity, piece_rows * SUB), jnp.float32)
        .at[slot_index]
        .set(piece_real)
    )
    send_imag = (
        jnp.zeros((col_devices * capacity, piece_rows * SUB), jnp.float32)
        .at[slot_index]
        .set(piece_imag)
    )
    send_start = jnp.zeros((col_devices * capacity,), jnp.int32).at[slot_index].set(starts)
    recv_real, recv_imag, recv_start = (
        lax.all_to_all(send_real, "col", split_axis=0, concat_axis=0, tiled=True),
        lax.all_to_all(send_imag, "col", split_axis=0, concat_axis=0, tiled=True),
        lax.all_to_all(send_start, "col", split_axis=0, concat_axis=0, tiled=True),
    )
    placed_real, placed_imag = place_blocks(
        recv_real,
        recv_imag,
        recv_start // tile_width,
        recv_start % tile_width,
        col_devices,
        tile_width,
    )
    widen = ((0, group_rows - piece_rows), (0, 0))
    slab_real = jnp.pad(placed_real.transpose(1, 0, 2).reshape(piece_rows, G), widen)
    slab_imag = jnp.pad(placed_imag.transpose(1, 0, 2).reshape(piece_rows, G), widen)
    rows_real, rows_imag = transform_last(slab_real, slab_imag, False)
    cols_real, cols_imag = (
        lax.all_to_all(
            lax.all_to_all(rows_real, "row", split_axis=1, concat_axis=0, tiled=True),
            "col",
            split_axis=1,
            concat_axis=0,
            tiled=True,
        ),
        lax.all_to_all(
            lax.all_to_all(rows_imag, "row", split_axis=1, concat_axis=0, tiled=True),
            "col",
            split_axis=1,
            concat_axis=0,
            tiled=True,
        ),
    )

    def reorder(field):
        return (
            field.reshape(col_devices, row_devices, group_rows, pencil_cols)
            .transpose(3, 1, 0, 2)
            .reshape(pencil_cols, G)
        )

    image = transform_last(reorder(cols_real), reorder(cols_imag), True) * (1.0 / G)
    halo_width = (KW - 1) // 2
    results = []
    padded = with_halo(image, ((("row", "col"), 0),), halo_width)
    for scale_index in range(NSCALE):
        vertical = smooth_along_rows(padded, scale_kernels[scale_index])
        results.append(smooth_across(vertical, scale_kernels[scale_index]))
    return jnp.stack(results)


def split(value):
    high = value.astype(BF16)
    return high, (value - high.astype(F32)).astype(BF16)


def split_table(table):
    table = np.asarray(table, np.float64)
    high = table.astype(BF16)
    return high, (table - high.astype(np.float64)).astype(BF16)


def turn(steps, length):
    angle = 2.0 * np.pi * (np.asarray(steps, np.int64) % length) / length
    return np.cos(angle), np.sin(angle)


def dot(left, right, left_dim=1, right_dim=0):
    return lax.dot_general(
        left, right, (((left_dim,), (right_dim,)), ((), ())), preferred_element_type=F32
    )


def dot3(left_high, left_low, right_high, right_low, left_dim=1, right_dim=0):
    return (
        dot(left_high, right_high, left_dim, right_dim)
        + dot(left_high, right_low, left_dim, right_dim)
        + dot(left_low, right_high, left_dim, right_dim)
    )


def subgrid_kernel(packed_ref, taps_ref, out_ref):
    span = 2 * VPS
    pairs = out_ref.shape[0] // SUB
    diagonal = lax.broadcasted_iota(jnp.int32, (OVER, SUP), 0) == lax.broadcasted_iota(
        jnp.int32, (OVER, SUP), 1
    )
    table = [
        jnp.sum(jnp.where(diagonal, taps_ref[s : s + 1, :], 0.0), axis=1, keepdims=True)
        for s in range(OVER)
    ]

    def taps(position):
        step = position & (OVER - 1)
        cell = position >> (OVER.bit_length() - 1)
        values = jnp.zeros((SUP, span), F32)
        for s in range(OVER):
            values = jnp.where(step == s, table[s], values)
        offset = lax.broadcasted_iota(jnp.int32, (SUB, span), 0) - cell
        result = jnp.zeros((SUB, span), F32)
        for t in range(SUP):
            result = jnp.where(offset == t, values[t : t + 1, :], result)
        return result

    first = lax.broadcasted_iota(jnp.int32, (SUB, LANES), 1) < LANES // 2

    def pair(p, carry):
        here = pl.ds(pl.multiple_of(p * span, span), span)
        along_rows = taps(packed_ref[2:3, here].astype(jnp.int32))
        along_cols = taps(packed_ref[3:4, here].astype(jnp.int32))
        weighted = jnp.concatenate(
            [along_rows * packed_ref[0:1, here], along_rows * packed_ref[1:2, here]], axis=0
        )
        weighted = jnp.concatenate(split(weighted), axis=0)
        cols = jnp.concatenate(split(along_cols), axis=0)
        sums = []
        for s in range(2):
            part = slice(s * VPS, (s + 1) * VPS)
            product = dot(cols[:, part], weighted[:, part], 1, 1)
            total = product[:SUB] + product[SUB:]
            sums.append(total + pltpu.roll(total, LANES // 2, 1))
        out_ref[pl.ds(pl.multiple_of(p * SUB, SUB), SUB), :] = jnp.where(first, sums[0], sums[1])
        return carry

    lax.fori_loop(0, pairs, pair, 0, unroll=8)


def radix_eight(real, imag):
    def four(r, i):
        a, b = (r[0] + r[2], i[0] + i[2])
        c, d = (r[0] - r[2], i[0] - i[2])
        e, f = (r[1] + r[3], i[1] + i[3])
        g, h = (r[1] - r[3], i[1] - i[3])
        return [(a + e, b + f), (c - h, d + g), (a - e, b - f), (c + h, d - g)]

    low = four(
        [real[n] + real[n + 4] for n in range(4)], [imag[n] + imag[n + 4] for n in range(4)]
    )
    dr = [real[n] - real[n + 4] for n in range(4)]
    di = [imag[n] - imag[n + 4] for n in range(4)]
    high = four(
        [dr[0], (dr[1] - di[1]) * ROOT_HALF, -di[2], (dr[3] + di[3]) * -ROOT_HALF],
        [di[0], (dr[1] + di[1]) * ROOT_HALF, dr[2], (dr[3] - di[3]) * ROOT_HALF],
    )
    return [(low, high)[c % 2][c // 2] for c in range(8)]


def row_kernel(info_ref, *refs, blocks, part, per_class, tile_width):
    xs = refs[:blocks]
    turn_ref, tables_ref = refs[blocks : blocks + 2]
    outs = refs[blocks + 2 : -6]
    real_ref, imag_ref, uh_ref, ul_ref, both_ref, sem = refs[-6:]
    fetch = pltpu.make_async_copy(tables_ref, both_ref, sem)
    fetch.start()
    rows = real_ref.shape[0]
    chunk = 256

    def clear(n, carry):
        here = pl.ds(pl.multiple_of(n * chunk, chunk), chunk)
        real_ref[here, :] = jnp.zeros((chunk, LANES), F32)
        imag_ref[here, :] = jnp.zeros((chunk, LANES), F32)
        return carry

    lax.fori_loop(0, rows // chunk, clear, 0)
    owner = lax.broadcasted_iota(jnp.int32, (SUB, LANES), 1) // SUB
    for b in range(blocks):
        pairs = xs[b].shape[0] // SUB

        def place(p, carry, b=b, pairs=pairs):
            piece = xs[b][pl.ds(pl.multiple_of(p * SUB, SUB), SUB), :]
            for s in range(2):
                number = 2 * p + s
                tile, group, start = (
                    info_ref[b, n * 2 * pairs + number].astype(jnp.int32) for n in range(3)
                )
                start = tile * tile_width + start
                for dest, at in ((real_ref, 2 * s), (imag_ref, 2 * s + 1)):
                    shift = (group * SUB + (LANES - at * SUB)) & (LANES - 1)
                    moved = jnp.where(owner == group, pltpu.roll(piece, shift, 1), 0.0)
                    dest[pl.ds(start, SUB), :] += moved
            return carry

        lax.fori_loop(0, pairs, place, 0, unroll=4)

    step = 16

    def classes(n, carry):
        first = pl.multiple_of(n * step, step)
        real = [real_ref[pl.ds(k * part + first, step), :] for k in range(RADIX)]
        imag = [imag_ref[pl.ds(k * part + first, step), :] for k in range(RADIX)]
        turns = turn_ref[pl.ds(first, step), :]
        for c, (ur, ui) in enumerate(radix_eight(real, imag)):
            cosine = turns[:, c : c + 1]
            sine = turns[:, RADIX + c : RADIX + c + 1]
            vr = ur * cosine - ui * sine
            vi = ur * sine + ui * cosine
            high, low = split(jnp.concatenate([vr, vi], axis=1))
            uh_ref[c, pl.ds(first, step), :] = high
            ul_ref[c, pl.ds(first, step), :] = low
        return carry

    lax.fori_loop(0, part // step, classes, 0, unroll=4)
    half = len(outs) * per_class
    fetch.wait()
    for c in range(RADIX):
        total = dot3(both_ref[0], both_ref[1], uh_ref[c], ul_ref[c])
        real = total[:half, :LANES] - total[half:, LANES:]
        imag = total[:half, LANES:] + total[half:, :LANES]
        here = slice(c * per_class, (c + 1) * per_class)
        for d, out_ref in enumerate(outs):
            mine = slice(d * per_class, (d + 1) * per_class)
            out_ref[here, :LANES] = real[mine]
            out_ref[here, LANES:] = imag[mine]


def band_kernel(taps_ref, across_ref, wrap_ref, inside_ref, out_ref, th_ref, tl_ref):
    def spread(index, scale):
        out = jnp.zeros(index.shape, F32)
        for u in range(KW):
            out = jnp.where(index == u, taps_ref[scale, u], out)
        return out

    across, wrap = across_ref[...], wrap_ref[...]
    rows = across.shape[0]
    for scale in range(NSCALE):
        cols = slice(scale * across.shape[1], (scale + 1) * across.shape[1])
        high, low = split(spread(across, scale) * inside_ref[...])
        out_ref[:rows, cols] = high
        out_ref[rows : 2 * rows, cols] = high
        out_ref[2 * rows :, cols] = low
        cols = slice(scale * wrap.shape[1], (scale + 1) * wrap.shape[1])
        th_ref[:, cols], tl_ref[:, cols] = split(spread(wrap, scale))


COS1, COS3 = math.cos(math.pi / 8), math.cos(3 * math.pi / 8)


def real_sixteen(h0, h8, x, y):
    a, b = h0 + h8, h0 - h8
    c, d = x[2] + x[6], (x[2] - x[6]) * ROOT_HALF
    even = [a + x[4] + c, b + d, a - x[4], b - d, a + x[4] - c]
    e, f = x[1] - x[7], x[3] - x[5]
    g, h = x[1] + x[7], x[3] + x[5]
    odd = [g + h, e * COS1 + f * COS3, (g - h) * ROOT_HALF, e * COS3 - f * COS1]
    cosines = [even[n] + odd[n] for n in range(4)] + [even[4]]
    cosines += [even[n] - odd[n] for n in (3, 2, 1, 0)]
    k = (y[2] + y[6]) * ROOT_HALF
    even = [None, k + y[4], y[2] - y[6], k - y[4]]
    e, f = y[1] + y[7], y[3] + y[5]
    odd = [
        None,
        e * COS3 + f * COS1,
        (y[1] - y[7] + y[3] - y[5]) * ROOT_HALF,
        e * COS1 - f * COS3,
        y[1] - y[7] - y[3] + y[5],
    ]
    sines = [None] + [even[n] + odd[n] for n in (1, 2, 3)] + [odd[4]]
    sines += [odd[n] - even[n] for n in (3, 2, 1)]
    out = [None] * 16
    out[0], out[8] = cosines[0], cosines[8]
    for n in range(1, 8):
        out[n] = cosines[n] - sines[n]
        out[16 - n] = cosines[n] + sines[n]
    return out


def column_kernel(
    row_ref, *refs,
):
    *parts, across_ref, hat_ref, th_ref, tl_ref, tables_ref = refs[:-11]
    out_ref, qt_ref, qh_ref, ql_ref, corr_ref, va_ref, vb_ref, o_ref, f_ref, sem, table_sem = refs[
        -11:
    ]
    tiles = tables_ref.shape[0] - 1
    fetches = [
        pltpu.make_async_copy(tables_ref.at[n], f_ref.at[n], table_sem.at[n])
        for n in range(tiles + 1)
    ]
    for fetch in fetches:
        fetch.start()
    bands = len(parts)
    width = qh_ref.shape[1]
    per_scale = width // NSCALE
    keys = LANES // 2
    half = CLASSES // 2

    for d, part in enumerate(parts):
        band = lax.rem(row_ref[0, 0] + (bands - d), bands)
        here = pl.ds(pl.multiple_of(band * LANES, LANES), LANES)
        high, low = split(part[...])
        product = dot(jnp.concatenate([high, low, high], axis=0), across_ref[...], 0, 0)
        for lane in range(width // LANES):
            cols = slice(lane * LANES, (lane + 1) * LANES)
            qt_ref[0, lane, here, :] = product[:LANES, cols]
            qt_ref[1, lane, here, :] = product[LANES:, cols]
    edge = jnp.zeros((width, LANES), F32)
    fetches[0].wait()
    for slot in range(half):
        halves = []
        for m in (slot, CLASSES - slot if slot else half):
            parts = []
            for lane in range(width // LANES):
                here = pl.ds(m, keys, stride=CLASSES)
                pair = [qt_ref[ri, lane, here, :] for ri in range(2)]
                parts.append(jnp.concatenate(pair, axis=0).T)
            halves.append(jnp.concatenate(parts, axis=0))
        high, low = split(jnp.concatenate(halves, axis=1))
        edge = edge + dot3(
            high, low, f_ref[0, 0, slot, :, :LANES], f_ref[0, 1, slot, :, :LANES]
        )
        for at, m in enumerate((slot, CLASSES - slot if slot else half)):
            q = halves[at]
            turned = pltpu.roll(q, keys, 1)
            lanes = slice(at * LANES, (at + 1) * LANES)
            for scale in range(NSCALE):
                mine = slice(scale * per_scale, (scale + 1) * per_scale)
                high, low = split(
                    q[mine] * hat_ref[scale, 0, m : m + 1, :]
                    + turned[mine] * hat_ref[scale, 1, m : m + 1, :]
                )
                qh_ref[slot, mine, lanes] = high
                ql_ref[slot, mine, lanes] = low
    high, low = split(edge)
    for scale in range(NSCALE):
        mine = slice(scale * per_scale, (scale + 1) * per_scale)
        cols = slice(scale * 2 * LANES, (scale + 1) * 2 * LANES)
        corr_ref[mine, :] = dot3(high[mine], low[mine], th_ref[:, cols], tl_ref[:, cols])

    def copy(tile, at):
        first = (at * tiles + tile) * LANES
        return pltpu.make_async_copy(
            o_ref.at[tile % 2, at], out_ref.at[:, first : first + LANES], sem.at[tile % 2, at]
        )

    step = 8

    def combine(v_ref, tile, first, last):
        for n in range(first, last, step):
            here = slice(n, n + step)
            x = [v_ref[m, here, :LANES] for m in range(half)]
            y = [v_ref[m, here, LANES:] for m in range(half)]
            outs = real_sixteen(x[0], y[0], x, y)
            if tile == 0:
                outs[0] = outs[0] - corr_ref[here, :LANES]
            if tile == tiles - 1:
                outs[-1] = outs[-1] - corr_ref[here, LANES:]
            for at in range(CLASSES):
                o_ref[tile % 2, at, here, :] = outs[at]

    share = width // half
    for tile in range(tiles + 1):
        now, before = (va_ref, vb_ref) if tile % 2 == 0 else (vb_ref, va_ref)
        if tile >= 3:
            for at in range(CLASSES):
                copy(tile - 3, at).wait()
        if tile < tiles:
            fetches[tile + 1].wait()
        for m in range(half):
            if tile < tiles:
                now[m] = dot3(
                    qh_ref[m], ql_ref[m], f_ref[tile + 1, 0, m], f_ref[tile + 1, 1, m]
                )
            if tile > 0:
                combine(before, tile - 1, m * share, (m + 1) * share)
        if tile > 0:
            for at in range(CLASSES):
                copy(tile - 1, at).start()
    for tile in range(max(tiles - 2, 0), tiles):
        for at in range(CLASSES):
            copy(tile, at).wait()


def kernel_device(
    vis, vis_pos, vis_w, subgrid_tile, subgrid_group, subgrid_col, grid_kernel, scale_kernels
):
    nr = lax.axis_size("row")
    nc = lax.axis_size("col")
    row, col = lax.axis_index("row"), lax.axis_index("col")
    tile_width = G // nc
    stride = G // nr
    cols_here = G // (nr * nc)
    window = cols_here + 2 * HALO
    per_class = window // RADIX
    part = G // RADIX
    subs = subgrid_col.shape[0]
    width = NSCALE * cols_here

    info = jnp.concatenate([subgrid_tile[:, 0], subgrid_group[:, 0], subgrid_col]).astype(F32)
    info = jnp.pad(info, (0, LANES - info.shape[0]))
    here = vis.shape[1]
    packed = jnp.concatenate(
        [
            jnp.concatenate(
                [jnp.stack(rotated_visibilities(vis, vis_w)), vis_pos.astype(F32)], axis=0
            ),
            jnp.broadcast_to(info[None], (4, LANES)),
        ],
        axis=1,
    )
    shifts = [[(i, (i + d) % nc) for i in range(nc)] for d in range(1, nc)]
    packs = [packed] + [lax.ppermute(packed, "col", s) for s in shifts]

    def grid_block(pack):
        return pl.pallas_call(
            subgrid_kernel,
            out_shape=jax.ShapeDtypeStruct((subs // 2 * SUB, LANES), F32),
            cost_estimate=pl.CostEstimate(
                flops=2 * 4 * subs * VPS * 4 * SUB * 2 * SUB,
                bytes_accessed=2**21,
                transcendentals=0,
            ),
            compiler_params=pltpu.CompilerParams(vmem_limit_bytes=32 * 2**20),
            name="subgrids",
        )(pack, grid_kernel)

    blocks = [grid_block(pack) for pack in packs[:2]]
    blocks[1], *packs[2:] = lax.optimization_barrier((blocks[1], *packs[2:]))
    blocks += [grid_block(pack) for pack in packs[2:]]
    infos = jnp.concatenate([pack[:1, here:] for pack in packs], axis=0)

    inner = np.arange(part)
    cosine, sine = turn(
        (stride * np.arange(nr)[:, None] + RADIX * np.arange(per_class)[None, :]).reshape(-1, 1)
        * inner,
        G,
    )
    tables = np.stack(split_table(np.concatenate([cosine, sine], axis=0)))
    first_q = (np.arange(nr)[:, None] * stride + np.arange(nc) * cols_here).reshape(-1, 1, 1) - HALO
    cosine, sine = turn((first_q + np.arange(RADIX)) * inner[None, :, None], G)
    turns = np.concatenate([cosine, sine], axis=2).astype(np.float32)
    turns = lax.dynamic_index_in_dim(jnp.asarray(turns), row * nc + col, 0, keepdims=False)
    vmem = pl.BlockSpec(memory_space=pltpu.VMEM)
    rows = pl.pallas_call(
        lambda *refs: row_kernel(
            *refs, blocks=nc, part=part, per_class=per_class, tile_width=tile_width
        ),
        out_shape=[jax.ShapeDtypeStruct((window, 2 * LANES), F32)] * nr,
        in_specs=[pl.BlockSpec(memory_space=pltpu.SMEM)]
        + [vmem] * (nc + 1)
        + [pl.BlockSpec(memory_space=pl.ANY)],
        out_specs=[vmem] * nr,
        scratch_shapes=[
            pltpu.VMEM((G, LANES), F32),
            pltpu.VMEM((G, LANES), F32),
            pltpu.VMEM((RADIX, part, 2 * LANES), BF16),
            pltpu.VMEM((RADIX, part, 2 * LANES), BF16),
            pltpu.VMEM(tables.shape, BF16),
            pltpu.SemaphoreType.DMA,
        ],
        compiler_params=pltpu.CompilerParams(vmem_limit_bytes=48 * 2**20),
        name="rows",
    )(infos, *blocks, turns, jnp.asarray(tables))

    rows = [rows[0]] + [
        lax.ppermute(rows[d], "row", [(i, (i + d) % nr) for i in range(nr)]) for d in range(1, nr)
    ]

    place = (RADIX * np.arange(per_class)[None, :] + np.arange(RADIX)[:, None]).reshape(-1)
    distance = place[:, None] - np.arange(cols_here)[None, :]
    distance = np.where((distance >= 0) & (distance < KW), distance, -1)
    at_q = (row * nc + col) * cols_here - HALO + jnp.asarray(place, jnp.int32)
    inside = ((at_q >= 0) & (at_q < G)).astype(F32) * (1.0 / G)
    wrap = np.full((LANES, 2 * LANES), -1)
    for e in range(HALO):
        for p in range(e + 1):
            wrap[e, p] = e - p
        for j in range(e, HALO):
            wrap[HALO + e, 2 * LANES - HALO + j] = e + 2 * HALO - j
    across, th, tl = pl.pallas_call(
        band_kernel,
        out_shape=[jax.ShapeDtypeStruct((3 * window, width), BF16)]
        + [jax.ShapeDtypeStruct((LANES, NSCALE * 2 * LANES), BF16)] * 2,
        in_specs=[pl.BlockSpec(memory_space=pltpu.SMEM)] + [vmem] * 3,
        out_specs=[vmem] * 3,
        compiler_params=pltpu.CompilerParams(vmem_limit_bytes=32 * 2**20),
        name="bands",
    )(
        scale_kernels,
        jnp.asarray(distance, jnp.int32),
        jnp.asarray(wrap, jnp.int32),
        inside[:, None],
    )
    per_band = LANES // CLASSES // nc
    keys = (
        np.arange(nr)[:, None, None] * stride
        + np.arange(nc)[None, :, None] * (stride // nc)
        + np.arange(per_band)[None, None, :] * CLASSES
    ).reshape(-1)
    k_of = np.arange(CLASSES)[:, None] + keys[None, :]
    cosine, sine = turn((np.arange(KW) - HALO)[:, None, None] * k_of, G)
    hat_table = np.stack(
        [
            np.concatenate([cosine, cosine], axis=2),
            np.concatenate([-sine, sine], axis=2),
        ],
        axis=1,
    )
    hat = jnp.dot(
        scale_kernels, jnp.asarray(hat_table.reshape(KW, -1), F32), precision=HIGHEST
    ).reshape(NSCALE, 2, CLASSES, 2 * keys.size)
    near = np.arange(-HALO, HALO)
    cosine, sine = turn(k_of[:, :, None] * near, G)
    edge = np.zeros((CLASSES, 2 * keys.size, 2 * LANES))
    edge[:, : keys.size, : 2 * HALO] = cosine
    edge[:, keys.size :, : 2 * HALO] = -sine
    half = CLASSES // 2
    others = [CLASSES - m if m else half for m in range(half)]
    edge = np.concatenate([edge[:half], edge[others]], axis=1)
    span = G // CLASSES
    tiles = span // LANES
    cosine, sine = turn(k_of[:, :, None] * np.arange(span), G)
    real = np.concatenate([cosine, -sine], axis=1)
    imag = np.concatenate([sine, cosine], axis=1)
    none = np.zeros_like(real[0])
    table = [np.block([[real[0], none], [none, real[half]]])]
    for m in range(1, half):
        other = CLASSES - m
        table.append(np.block([[real[m], imag[m]], [real[other], -imag[other]]]))
    table = np.stack(table).reshape(half, 4 * keys.size, 2, tiles, LANES)
    table = table.transpose(3, 0, 1, 2, 4).reshape(tiles, half, 4 * keys.size, 2 * LANES)
    tables = np.stack(split_table(np.concatenate([edge[None], table], axis=0)), axis=1)
    operands = (*rows, across, hat, th, tl)
    out = pl.pallas_call(
        column_kernel,
        out_shape=jax.ShapeDtypeStruct((width, G), F32),
        in_specs=[pl.BlockSpec(memory_space=pltpu.SMEM)]
        + [vmem] * len(operands)
        + [pl.BlockSpec(memory_space=pl.ANY)],
        out_specs=pl.BlockSpec(memory_space=pl.ANY),
        scratch_shapes=[
            pltpu.VMEM((2, width // LANES, nr * LANES, LANES), F32),
            pltpu.VMEM((half, width, 4 * keys.size), BF16),
            pltpu.VMEM((half, width, 4 * keys.size), BF16),
            pltpu.VMEM((width, 2 * LANES), F32),
            pltpu.VMEM((half, width, 2 * LANES), F32),
            pltpu.VMEM((half, width, 2 * LANES), F32),
            pltpu.VMEM((2, CLASSES, width, LANES), F32),
            pltpu.VMEM(tables.shape, BF16),
            pltpu.SemaphoreType.DMA((2, CLASSES)),
            pltpu.SemaphoreType.DMA((tables.shape[0],)),
        ],
        compiler_params=pltpu.CompilerParams(vmem_limit_bytes=52 * 2**20),
        name="columns",
    )(row.astype(jnp.int32).reshape(1, 1), *operands, jnp.asarray(tables))
    return out.reshape(NSCALE, cols_here, G)


def solution(mesh):
    nr, nc = mesh.shape["row"], mesh.shape["col"]
    fits = nr == RADIX and nc * SUB == LANES
    return jax.shard_map(
        kernel_device if fits else general_device,
        mesh=mesh,
        in_specs=(
            P(None, ("row", "col")),
            P(None, ("row", "col")),
            P(("row", "col")),
            P(("row", "col"), None),
            P(("row", "col"), None),
            P(("row", "col")),
            P(),
            P(),
        ),
        out_specs=P(None, ("row", "col"), None),
        check_vma=False,
    )
```
